256 devices in a mesh: lat: 8 (over x, core), lon: 32 (over z, y).
Axes of the slice: x: 4, y: 4, z: 8, core: 2. Of those that a mesh axis runs over, the one named last changes fastest.
Arguments:
- fields: bfloat16 [4, 32, 288, 1024], P(None, 'lat', 'lon'), may hold values from -6 to 6
- conv_first: float32 [9, 1024], replicated, may hold values from -2 to 2
- w_qkv: bfloat16 [1024, 3072], replicated, may hold values from -2 to 2
- w_out: bfloat16 [1024, 1024], replicated, may hold values from -0.1875 to 0.1875
- conv_second: float32 [9, 1024], replicated, may hold values from -2 to 2
- key_list: int32 [8, 32, 32], P('lat', 'lon'), may hold values from 0 to 31, as said below
- key_count: int32 [8, 32], P('lat', 'lon'), may hold values from 1 to 32, as said below
Outputs:
- attended: bfloat16 [4, 32, 288, 1024], P(None, 'lat', 'lon')
- mixed: bfloat16 [4, 32, 288, 1024], P(None, 'lat', 'lon')
The draws below stay inside these ranges and needn't reach their ends.
Inputs may be any that keep to these rules, and one draw needn't show every extreme that they name: Entry 0 of key_list[p, q] is q; entries 1 to key_count[p, q] - 1 are distinct longitude band indices other than q; the remaining entries are q. key_count[p, q] is 32 in the first and the last latitude band.
All inputs are finite; a program needn't handle non-finite values.
Results may differ from the reference program's by a relative error of at most 0.034.
Values may be sent and summed in bfloat16 or wider, within the bound.
A program may use at most 128 MiB of HBM per device.

```python
import jax
import jax.numpy as jnp
from jax import lax

D = 1024
HEADS = 16
HEAD = 64
LEVELS = 4
ROWS_DEV = 4
COLS_DEV = 9
TOK_DEV = 144
LAT_BLOCKS = 8
LON_BLOCKS = 32
LAT_ROWS = 32
LON_COLS = 288


def draw_fields(key, part):
    values = jax.random.normal(key, (LEVELS, LAT_ROWS, LON_COLS, D), jnp.float32)
    return jnp.clip(values, -6.0, 6.0).astype(jnp.bfloat16)


def draw_w_qkv(key, part):
    factor = D ** (-0.5)
    w_query = jax.random.normal(jax.random.fold_in(key, 1), (D, D), jnp.float32) * factor
    w_key = jax.random.normal(jax.random.fold_in(key, 2), (D, D), jnp.float32) * factor
    w_value = jax.random.normal(jax.random.fold_in(key, 3), (D, D), jnp.float32) * factor
    query_out = w_query * 1.6
    key_out = w_key * 1.6
    return jnp.concatenate([query_out, key_out, w_value], axis=1).astype(jnp.bfloat16)


def teleconnections(key):
    band_index = jnp.arange(LAT_BLOCKS, dtype=jnp.int32)[:, None]
    distance = jnp.minimum(band_index, LAT_BLOCKS - 1 - band_index)
    half_bands = max(1, LAT_BLOCKS // 2)
    ceiling = jnp.clip((LON_BLOCKS * (half_bands - distance) + half_bands - 1) // half_bands, 2, LON_BLOCKS)
    ceiling = jnp.broadcast_to(ceiling, (LAT_BLOCKS, LON_BLOCKS))
    counts = jax.random.randint(jax.random.fold_in(key, 11), (LAT_BLOCKS, LON_BLOCKS), 1, ceiling + 1)
    counts = jnp.where(jnp.broadcast_to(distance, (LAT_BLOCKS, LON_BLOCKS)) == 0, LON_BLOCKS, counts).astype(jnp.int32)
    scores = jax.random.randint(jax.random.fold_in(key, 12), (LAT_BLOCKS, LON_BLOCKS, LON_BLOCKS - 1), 0, 1 << 20)
    scores = scores * (LON_BLOCKS - 1) + jnp.arange(LON_BLOCKS - 1, dtype=jnp.int32)
    order = jnp.argsort(scores, axis=-1, stable=True).astype(jnp.int32)
    own = jnp.broadcast_to(jnp.arange(LON_BLOCKS, dtype=jnp.int32)[None, :, None], (LAT_BLOCKS, LON_BLOCKS, 1))
    others = (own + order + 1) % LON_BLOCKS
    listed = jnp.concatenate([own, others], axis=-1)
    slot_index = jnp.arange(LON_BLOCKS, dtype=jnp.int32)
    listed = jnp.where(slot_index[None, None, :] < counts[..., None], listed, own)
    return (listed.astype(jnp.int32), counts)


def draw_key_list(key, part):
    return teleconnections(key)[0]


def draw_key_count(key, part):
    return teleconnections(key)[1]


def centred(own_key, shape, spread, bound, kind=jnp.bfloat16):
    entries = jax.random.normal(own_key, shape, jnp.float32) * spread
    return jnp.minimum(jnp.maximum(entries, -bound), bound).astype(kind)


def setup_inputs(seed: int = 0) -> dict:
    arg_keys = jax.random.split(jax.random.key(seed), 8)
    fields = draw_fields(jax.random.fold_in(arg_keys[7], 71), 0)
    conv_first = centred(arg_keys[1], (9, D), 9 ** -0.5, 2.0, jnp.float32)
    w_qkv = draw_w_qkv(jax.random.fold_in(arg_keys[7], 71), 0)
    w_out = centred(arg_keys[3], (D, D), D ** -0.5, 0.1875)
    conv_second = centred(arg_keys[4], (9, D), 9 ** -0.5, 2.0, jnp.float32)
    key_list = draw_key_list(jax.random.fold_in(arg_keys[7], 71), 0)
    key_count = draw_key_count(jax.random.fold_in(arg_keys[7], 71), 0)
    return dict(fields=fields, conv_first=conv_first, w_qkv=w_qkv, w_out=w_out, conv_second=conv_second, key_list=key_list, key_count=key_count)


NEG_FILL = -1e+30
EPSILON = 1e-05

def depthwise(field, weights):
    row_count = field.shape[1]
    column_count = field.shape[2]
    widened = field.astype(jnp.float32)
    widened = jnp.concatenate([widened[:, :, -1:], widened, widened[:, :, :1]], axis=2)
    widened = jnp.pad(widened, ((0, 0), (1, 1), (0, 0), (0, 0)))
    result = jnp.zeros(field.shape, jnp.float32)
    for offset_lat in range(3):
        for offset_lon in range(3):
            result = result + weights[3 * offset_lat + offset_lon] * widened[:, offset_lat:offset_lat + row_count, offset_lon:offset_lon + column_count]
    return result

def to_blocks(array):
    shaped = array.reshape(LEVELS, LAT_BLOCKS, ROWS_DEV, LON_BLOCKS, COLS_DEV, array.shape[-1])
    return shaped.transpose(1, 3, 0, 2, 4, 5).reshape(LAT_BLOCKS, LON_BLOCKS, TOK_DEV, array.shape[-1])

def attend_all(query, keyvals, valid):
    queries = query.astype(jnp.float32).reshape(TOK_DEV, HEADS, HEAD)
    keys_part = keyvals[:, :D].astype(jnp.float32).reshape(-1, HEADS, HEAD)
    values_part = keyvals[:, D:].astype(jnp.float32).reshape(-1, HEADS, HEAD)
    scores = jnp.einsum('qhd,khd->qhk', queries, keys_part) * HEAD ** (-0.5)
    scores = jnp.where(valid[None, None, :], scores, NEG_FILL)
    highest = lax.optimization_barrier(jnp.max(scores, axis=-1, keepdims=True))
    weights = jnp.where(valid[None, None, :], jnp.exp(scores - highest), 0.0)
    summed = lax.optimization_barrier(jnp.sum(weights, axis=-1))
    rounded = lax.optimization_barrier(weights.astype(jnp.bfloat16)).astype(jnp.float32)
    result = jnp.einsum('qhk,khd->qhd', rounded, values_part) / summed[..., None]
    return result.reshape(TOK_DEV, D).astype(jnp.bfloat16)

def reference(fields, conv_first, w_qkv, w_out, conv_second, key_list, key_count):
    stream = (fields.astype(jnp.float32) + depthwise(fields, conv_first)).astype(jnp.bfloat16)
    flat = stream.reshape(-1, D).astype(jnp.float32)
    normed = (flat * lax.rsqrt(lax.optimization_barrier(jnp.mean(flat * flat, axis=-1, keepdims=True)) + EPSILON)).astype(jnp.bfloat16)
    packed = jnp.dot(normed, w_qkv, preferred_element_type=jnp.float32).astype(jnp.bfloat16)
    blocks = to_blocks(packed)
    queries = blocks[..., :D]
    keyvals = blocks[..., D:]
    slot_index = jnp.arange(LON_BLOCKS, dtype=jnp.int32)

    def one_block(index):
        lat_band = index // LON_BLOCKS
        lon_band = index % LON_BLOCKS
        query = queries[lat_band, lon_band]
        band = keyvals[lat_band].reshape(LON_BLOCKS * TOK_DEV, 2 * D)
        upper = keyvals[jnp.maximum(lat_band - 1, 0), lon_band]
        lower = keyvals[jnp.minimum(lat_band + 1, LAT_BLOCKS - 1), lon_band]
        keys_all = jnp.concatenate([band, upper, lower], axis=0)
        listed = key_list[lat_band, lon_band]
        used = slot_index < key_count[lat_band, lon_band]
        linked = jnp.any((listed[None, :] == slot_index[:, None]) & used[None, :], axis=1)
        valid = jnp.concatenate([jnp.repeat(linked, TOK_DEV), jnp.full((TOK_DEV,), lat_band > 0), jnp.full((TOK_DEV,), lat_band < LAT_BLOCKS - 1)])
        return attend_all(query, keys_all, valid)
    outputs = lax.map(one_block, jnp.arange(LAT_BLOCKS * LON_BLOCKS, dtype=jnp.int32))
    outputs = outputs.reshape(LAT_BLOCKS, LON_BLOCKS, LEVELS, ROWS_DEV, COLS_DEV, D)
    attended = outputs.transpose(2, 0, 3, 1, 4, 5).reshape(LEVELS, LAT_ROWS, LON_COLS, D)
    projected = jnp.dot(attended.reshape(-1, D), w_out, preferred_element_type=jnp.float32)
    after = (flat_stream_f32(stream) + projected).astype(jnp.bfloat16).reshape(fields.shape)
    mixed = (after.astype(jnp.float32) + depthwise(after, conv_second)).astype(jnp.bfloat16)
    return (attended, mixed)

def flat_stream_f32(stream):
    return stream.reshape(-1, D).astype(jnp.float32)
```

```python
import functools
import math

import jax
import jax.numpy as jnp
from jax import lax
from jax.experimental import pallas as pl
from jax.experimental.pallas import tpu as pltpu
from jax.sharding import PartitionSpec as P

LEVELS, ROWS, COLS = 4, 4, 9
TOK = LEVELS * ROWS * COLS
HEAD = 64
LANES = 128
MSG = 3 * TOK + 16
EPSILON = 1e-05
NEG = -1e30
LOW = -3e38
MESH = pl.DeviceIdType.MESH
F32, BF16 = jnp.float32, jnp.bfloat16

SIDES = (
    (-1, 0, 0, 48),
    (1, 0, 48, 48),
    (0, -1, 96, 16),
    (0, 1, 112, 16),
    (-1, -1, 128, 16),
    (-1, 1, 144, 16),
    (1, -1, 160, 16),
    (1, 1, 176, 16),
)
OPPOSITE = (1, 0, 3, 2, 7, 6, 5, 4)
HALO_ROWS = 192


def cells_of(a, b):
    rows = {-1: [1], 1: [ROWS], 0: list(range(1, ROWS + 1))}[a]
    cols = {-1: [1], 1: [COLS], 0: list(range(1, COLS + 1))}[b]
    rim = [(r, c) for r in rows for c in cols]
    return rim, [(r + a, c + b) for r, c in rim]


def kernel(
    nlat, nz, ny,
    fields, conv_a, conv_b, key_list, key_count, w_qkv, w_out,
    att_out, mix_out,
    wq, wo, flat, grid, stream, stage, halo_f, halo_send, halo_recv,
    send_buf, recv_buf, gath, near, qx, kx, vx, acc, top, back_send, back_recv,
    w_sem, hs_sem, hr_sem, zs_sem, zr_sem, ys_sem, yr_sem, rs_sem, rr_sem, ls_sem, lr_sem, bs_sem, br_sem,
):
    lat = lax.axis_index("lat")
    lon = lax.axis_index("lon")
    z = lon // ny
    y = lon % ny
    nlon = nz * ny
    width = nz * LANES
    has_north = lat > 0
    has_south = lat < nlat - 1

    def wrap(i, n):
        return lax.rem(i + n, n)

    def at(zz, yy):
        return (lat, zz * ny + yy)

    wq_copy = pltpu.make_async_copy(w_qkv, wq, w_sem.at[0])
    wo_copy = pltpu.make_async_copy(w_out, wo, w_sem.at[1])
    wq_copy.start()
    wo_copy.start()

    barrier = pltpu.get_barrier_semaphore()

    def greet(dev):
        pl.semaphore_signal(barrier, inc=1, device_id=dev, device_id_type=MESH)

    for k in range(1, nz):
        greet(at(wrap(z + k, nz), y))
    greet(at(z, wrap(y + 1, ny)))
    greet(at(z, wrap(y - 1, ny)))
    greet((lat, wrap(lon + 1, nlon)))
    greet((lat, wrap(lon - 1, nlon)))

    @pl.when(has_north)
    def _():
        for d in (-1, 0, 1):
            greet((lat - 1, wrap(lon + d, nlon)))

    @pl.when(has_south)
    def _():
        for d in (-1, 0, 1):
            greet((lat + 1, wrap(lon + d, nlon)))

    for l in range(LEVELS):
        for r in range(ROWS):
            cells = fields[l, r].astype(F32)
            for t in range(nz):
                flat[t, pl.ds((l * ROWS + r) * 16, COLS), :] = cells[:, t * LANES : (t + 1) * LANES]
    for r in range(ROWS):
        for c in range(COLS):
            for t in range(nz):
                grid[r + 1, c + 1, 0:LEVELS, t * LANES : (t + 1) * LANES] = flat[
                    t, pl.ds(r * 16 + c, LEVELS, stride=ROWS * 16), :
                ]

    def exists(a):
        return {-1: has_north, 0: None, 1: has_south}[a]

    def maybe(cond, fn):
        if cond is None:
            fn()
        else:
            pl.when(cond)(fn)

    def halo_copy(which, i):
        a, b, first, rows = SIDES[i]
        first_there = SIDES[OPPOSITE[i]][2]
        return pltpu.make_async_remote_copy(
            src_ref=halo_send.at[which, pl.ds(first, rows)],
            dst_ref=halo_recv.at[which, pl.ds(first_there, rows)],
            send_sem=hs_sem.at[which, i],
            recv_sem=hr_sem.at[which, OPPOSITE[i]],
            device_id=(lat + a, wrap(lon + b, nlon)),
            device_id_type=MESH,
        )

    def halo_wait(which, i):
        a, b, first, rows = SIDES[i]
        return pltpu.make_async_remote_copy(
            src_ref=halo_send.at[which, pl.ds(first, rows)],
            dst_ref=halo_recv.at[which, pl.ds(first, rows)],
            send_sem=hs_sem.at[which, i],
            recv_sem=hr_sem.at[which, i],
            device_id=(lat + a, wrap(lon + b, nlon)),
            device_id_type=MESH,
        )

    def halo_start(which):
        for i, (a, b, first, rows) in enumerate(SIDES):
            rim, _ = cells_of(a, b)
            for n, (r, c) in enumerate(rim):
                halo_f[pl.ds(first + 4 * n, 4), :] = grid[r, c, 0:LEVELS, :]
            halo_send[which, pl.ds(first, rows), :] = halo_f[pl.ds(first, rows), :].astype(BF16)
            maybe(exists(a), lambda: halo_copy(which, i).start())

    def halo_end(which):
        for i, (a, b, first, rows) in enumerate(SIDES):
            maybe(exists(a), lambda: halo_wait(which, i).wait_recv())
            halo_f[pl.ds(first, rows), :] = halo_recv[which, pl.ds(first, rows), :].astype(F32)
            _, beyond = cells_of(a, b)
            for n, (r, c) in enumerate(beyond):
                value = halo_f[pl.ds(first + 4 * n, 4), :]
                if a != 0:
                    value = jnp.where(exists(a), value, 0.0)
                grid[r, c, 0:LEVELS, :] = value

    def conv(weights, dst):
        chunk = min(256, width)
        for first in range(0, width, chunk):
            lanes = slice(first, first + chunk)
            w = weights[:, lanes]
            for r in range(ROWS):
                total = grid[r + 1, 1 : COLS + 1, 0:LEVELS, lanes]
                for a in range(3):
                    for b in range(3):
                        total = total + w[3 * a + b][None, None, :] * grid[r + a, b : b + COLS, 0:LEVELS, lanes]
                total = total.astype(BF16).astype(F32)
                for c in range(COLS):
                    for t in range(chunk // LANES):
                        dst[first // LANES + t, pl.ds((r * COLS + c) * LEVELS, LEVELS), :] = total[
                            c, :, t * LANES : (t + 1) * LANES
                        ]

    greetings = nz - 1 + 4 + 3 * has_north.astype(jnp.int32) + 3 * has_south.astype(jnp.int32)
    halo_f[...] = jnp.zeros_like(halo_f)
    pl.semaphore_wait(barrier, greetings)
    halo_start(0)

    lane = lax.broadcasted_iota(jnp.int32, (16, LANES), 1)
    count = key_count[0, 0]
    seen = ((lane == nlon) & has_north) | ((lane == nlon + 1) & has_south)
    for s in range(nlon):
        seen = seen | (lane == jnp.where(s < count, key_list[0, 0, s], -1))
    bias = jnp.where(seen, 0.0, NEG).astype(BF16)
    for k in range(nz):
        send_buf[k, pl.ds(3 * TOK, 16), :] = bias

    halo_end(0)
    conv(conv_a, stream)

    def tokens(ref):
        return jnp.concatenate([ref[t] for t in range(nz)], axis=1)

    def keep(ref, value):
        for t in range(nz):
            ref[t] = value[:, t * LANES : (t + 1) * LANES]

    x = tokens(stream)
    normed = (x * lax.rsqrt(jnp.mean(x * x, axis=-1, keepdims=True) + EPSILON)).astype(BF16)
    wq_copy.wait()

    def z_copy(k):
        there = wrap(z + k, nz)
        return pltpu.make_async_remote_copy(
            src_ref=send_buf.at[there],
            dst_ref=recv_buf.at[k],
            send_sem=zs_sem.at[k],
            recv_sem=zr_sem.at[k],
            device_id=at(there, y),
            device_id_type=MESH,
        )

    scale = HEAD ** -0.5 * math.log2(math.e)
    npair = nz // 2
    pair = z // 2
    order = [npair // 2] + [o for o in range(1, npair) if o != npair // 2] + [0]
    for off in order:
        j = wrap(pair + off, npair)
        for part in range(3):
            cols = pl.ds(pl.multiple_of(part * width + j * 256, 256), 256)
            res = jnp.dot(normed, wq[:, cols], preferred_element_type=F32)
            if part == 0:
                res = res * scale
            res = res.astype(BF16)
            send_buf[2 * j, pl.ds(part * TOK, TOK), :] = res[:, :LANES]
            send_buf[2 * j + 1, pl.ds(part * TOK, TOK), :] = res[:, LANES:]
        for half in range(2):
            k = wrap(2 * j + half - z, nz)

            @pl.when(k != 0)
            def _():
                z_copy(k).start()

    recv_buf[0] = send_buf[z]

    def y_copy(way, k):
        return pltpu.make_async_remote_copy(
            src_ref=recv_buf.at[k, pl.ds(TOK, 2 * TOK)],
            dst_ref=gath.at[way, k],
            send_sem=ys_sem.at[way, k],
            recv_sem=yr_sem.at[way, k],
            device_id=at(z, wrap(y + 1 - 2 * way, ny)),
            device_id_type=MESH,
        )

    def relay_copy(way, k):
        rows = pl.ds(way * TOK, TOK)
        return pltpu.make_async_remote_copy(
            src_ref=gath.at[way, k, rows],
            dst_ref=gath.at[2, k, rows],
            send_sem=rs_sem.at[way, k],
            recv_sem=rr_sem.at[way, k],
            device_id=at(z, wrap(y + 1 - 2 * way, ny)),
            device_id_type=MESH,
        )

    def lat_copy(way, k):
        return pltpu.make_async_remote_copy(
            src_ref=recv_buf.at[k, pl.ds(TOK, 2 * TOK)],
            dst_ref=near.at[1 - way, k],
            send_sem=ls_sem.at[way, k],
            recv_sem=lr_sem.at[1 - way, k],
            device_id=(lat - 1 + 2 * way, lon),
            device_id_type=MESH,
        )

    def lat_wait(side, k):
        return pltpu.make_async_remote_copy(
            src_ref=recv_buf.at[k, pl.ds(TOK, 2 * TOK)],
            dst_ref=near.at[side, k],
            send_sem=ls_sem.at[side, k],
            recv_sem=lr_sem.at[side, k],
            device_id=(lat - 1 + 2 * side, lon),
            device_id_type=MESH,
        )

    def forward(k, carry):
        @pl.when(k > 0)
        def _():
            z_copy(k).wait_recv()

        y_copy(0, k).start()
        y_copy(1, k).start()

        @pl.when(has_north)
        def _():
            lat_copy(0, k).start()

        @pl.when(has_south)
        def _():
            lat_copy(1, k).start()

        return carry

    lax.fori_loop(0, nz, forward, 0)

    lane_t = lax.broadcasted_iota(jnp.int32, (TOK, LANES), 1)

    def prepare(k, carry):
        q = recv_buf[k, pl.ds(0, TOK), :]
        b = jnp.concatenate([recv_buf[k, pl.ds(3 * TOK, 16), :]] * (TOK // 16), axis=0)
        zero = jnp.zeros_like(q)
        qx[k, pl.ds(0, TOK), 0:LANES] = jnp.where(lane_t < HEAD, q, zero)
        qx[k, pl.ds(TOK, TOK), 0:LANES] = jnp.where(lane_t < HEAD, zero, q)
        qx[k, pl.ds(0, TOK), LANES:] = b
        qx[k, pl.ds(TOK, TOK), LANES:] = b
        top[k] = jnp.full((2 * TOK, LANES), LOW, F32)
        acc[k] = jnp.zeros((2 * TOK, 2 * LANES), F32)
        return carry

    lax.fori_loop(0, nz, prepare, 0)

    def relay(k, carry):
        for way in range(2):
            y_copy(way, k).wait_recv()
            relay_copy(way, k).start()
        return carry

    lax.fori_loop(0, nz, relay, 0)

    ones = jnp.ones((TOK, LANES), BF16)

    def attend(k, keys, values):
        s = lax.dot_general(qx[k], keys, (((1,), (1,)), ((), ())), preferred_element_type=F32)
        old = top[k]
        new = jnp.maximum(old, jnp.max(s, axis=1, keepdims=True))
        p = jnp.exp2(s - new[:, :1]).astype(BF16)
        pv = jnp.dot(p, values, preferred_element_type=F32)
        factor = jnp.exp2(old - new)
        acc[k] = acc[k] * jnp.concatenate([factor, factor], axis=1) + pv
        top[k] = new

    def fill(n, number, block):
        rows = pl.ds(pl.multiple_of(n * TOK, 16), TOK)
        kx[rows, 0:LANES] = block[0]
        kx[rows, LANES:] = jnp.where(lane_t == number, 1.0, 0.0).astype(BF16)
        vx[rows, 0:LANES] = block[1]

    for n in range(nz):
        vx[pl.ds(n * TOK, TOK), LANES:] = ones

    def band(read, y0):
        def put(k, carry):
            fill(k, wrap(z - k, nz) * ny + y0, read(k))
            return carry

        lax.fori_loop(0, nz, put, 0)

        def step(k, carry):
            attend(k, kx[...], vx[...])
            return carry

        lax.fori_loop(0, nz, step, 0)

    band(lambda k: (recv_buf[k, pl.ds(TOK, TOK), :], recv_buf[k, pl.ds(2 * TOK, TOK), :]), y)
    for way in range(2):
        band(lambda k: (gath[way, k, pl.ds(0, TOK), :], gath[way, k, pl.ds(TOK, TOK), :]), wrap(y - 1 + 2 * way, ny))

    def relay_wait(k, carry):
        relay_copy(0, k).wait_recv()
        relay_copy(1, k).wait_recv()
        return carry

    lax.fori_loop(0, nz, relay_wait, 0)
    band(lambda k: (gath[2, k, pl.ds(0, TOK), :], gath[2, k, pl.ds(TOK, TOK), :]), wrap(y + 2, ny))

    def back_copy(k):
        there = wrap(z - k, nz)
        return pltpu.make_async_remote_copy(
            src_ref=back_send.at[k],
            dst_ref=back_recv.at[z],
            send_sem=bs_sem.at[k],
            recv_sem=br_sem.at[k],
            device_id=at(there, y),
            device_id_type=MESH,
        )

    def back_wait(k):
        there = wrap(z + k, nz)
        return pltpu.make_async_remote_copy(
            src_ref=back_send.at[k],
            dst_ref=back_recv.at[there],
            send_sem=bs_sem.at[k],
            recv_sem=br_sem.at[k],
            device_id=at(there, y),
            device_id_type=MESH,
        )

    def finish(k, carry):
        for side, cond in ((0, has_north), (1, has_south)):

            @pl.when(cond)
            def _():
                lat_wait(side, k).wait_recv()

            there = cond
            block = [jnp.where(there, near[side, k, pl.ds(i * TOK, TOK), :], jnp.zeros((TOK, LANES), BF16)) for i in range(2)]
            fill(side, nlon + side, block)
        attend(k, kx[pl.ds(0, 2 * TOK), :], vx[pl.ds(0, 2 * TOK), :])
        result = acc[k]
        result = result[:, :LANES] / result[:, LANES:]
        result = jnp.where(lane_t < HEAD, result[:TOK], result[TOK:]).astype(BF16)

        @pl.when(k == 0)
        def _():
            back_recv[z] = result

        @pl.when(k > 0)
        def _():
            back_send[k] = result
            back_copy(k).start()

        return carry

    lax.fori_loop(0, nz, finish, 0)
    for k in range(1, nz):
        back_wait(k).wait_recv()

    attended = jnp.concatenate([back_recv[k] for k in range(nz)], axis=1)
    wo_copy.wait()
    after = tokens(stream) + jnp.dot(attended, wo[...], preferred_element_type=F32)
    keep(stage, after.astype(BF16).astype(F32))
    for r in range(ROWS):
        for c in range(COLS):
            for t in range(nz):
                grid[r + 1, c + 1, 0:LEVELS, t * LANES : (t + 1) * LANES] = stage[
                    t, pl.ds((r * COLS + c) * LEVELS, LEVELS), :
                ]
    halo_start(1)
    keep(stage, attended.astype(F32))

    def leave(out):
        for l in range(LEVELS):
            for r in range(ROWS):
                for t in range(nz):
                    out[l, r, :, t * LANES : (t + 1) * LANES] = stage[
                        t, pl.ds(r * COLS * LEVELS + l, COLS, stride=LEVELS), :
                    ].astype(BF16)

    leave(att_out)
    halo_end(1)
    conv(conv_b, stage)
    leave(mix_out)

    for which in range(2):
        for i, (a, b, first, rows) in enumerate(SIDES):
            maybe(exists(a), lambda: halo_copy(which, i).wait_send())

    def sent(k, carry):
        @pl.when(k > 0)
        def _():
            z_copy(k).wait_send()
            back_copy(k).wait_send()

        for way in range(2):
            y_copy(way, k).wait_send()
            relay_copy(way, k).wait_send()

        @pl.when(has_north)
        def _():
            lat_copy(0, k).wait_send()

        @pl.when(has_south)
        def _():
            lat_copy(1, k).wait_send()

        return carry

    lax.fori_loop(0, nz, sent, 0)


def local(nlat, nz, ny, fields, conv_first, w_qkv, w_out, conv_second, key_list, key_count):
    width = fields.shape[-1]
    vmem = pl.BlockSpec(memory_space=pltpu.VMEM)
    smem = pl.BlockSpec(memory_space=pltpu.SMEM)
    hbm = pl.BlockSpec(memory_space=pl.ANY)
    dma = pltpu.SemaphoreType.DMA
    out = jax.ShapeDtypeStruct(fields.shape, BF16)
    return pl.pallas_call(
        functools.partial(kernel, nlat, nz, ny),
        out_shape=(out, out),
        in_specs=[vmem, vmem, vmem, smem, smem, hbm, hbm],
        out_specs=(vmem, vmem),
        scratch_shapes=[
            pltpu.VMEM(w_qkv.shape, BF16),
            pltpu.VMEM(w_out.shape, BF16),
            pltpu.VMEM((nz, LEVELS * ROWS * 16, LANES), F32),
            pltpu.VMEM((ROWS + 2, COLS + 2, 8, width), F32),
            pltpu.VMEM((nz, TOK, LANES), F32),
            pltpu.VMEM((nz, TOK, LANES), F32),
            pltpu.VMEM((HALO_ROWS, width), F32),
            pltpu.VMEM((2, HALO_ROWS, width), BF16),
            pltpu.VMEM((2, HALO_ROWS, width), BF16),
            pltpu.VMEM((nz, MSG, LANES), BF16),
            pltpu.VMEM((nz, MSG, LANES), BF16),
            pltpu.VMEM((3, nz, 2 * TOK, LANES), BF16),
            pltpu.VMEM((2, nz, 2 * TOK, LANES), BF16),
            pltpu.VMEM((nz, 2 * TOK, 2 * LANES), BF16),
            pltpu.VMEM((nz * TOK, 2 * LANES), BF16),
            pltpu.VMEM((nz * TOK, 2 * LANES), BF16),
            pltpu.VMEM((nz, 2 * TOK, 2 * LANES), F32),
            pltpu.VMEM((nz, 2 * TOK, LANES), F32),
            pltpu.VMEM((nz, TOK, LANES), BF16),
            pltpu.VMEM((nz, TOK, LANES), BF16),
            dma((2,)),
            dma((2, 8)),
            dma((2, 8)),
            dma((nz,)),
            dma((nz,)),
            dma((2, nz)),
            dma((2, nz)),
            dma((2, nz)),
            dma((2, nz)),
            dma((2, nz)),
            dma((2, nz)),
            dma((nz,)),
            dma((nz,)),
        ],
        compiler_params=pltpu.CompilerParams(
            collective_id=0, has_side_effects=True, vmem_limit_bytes=56 * 1024 * 1024
        ),
        name="block",
    )(fields, conv_first, conv_second, key_list, key_count, w_qkv, w_out)


def solution(mesh):
    nlat, nlon = mesh.shape["lat"], mesh.shape["lon"]
    nz = 8
    return jax.shard_map(
        functools.partial(local, nlat, nz, nlon // nz),
        mesh=mesh,
        in_specs=(
            P(None, "lat", "lon", None),
            P(),
            P(),
            P(),
            P(),
            P("lat", "lon", None),
            P("lat", "lon"),
        ),
        out_specs=(P(None, "lat", "lon", None), P(None, "lat", "lon", None)),
        check_vma=False,
    )
```

```python
import functools
import math

import jax
import jax.numpy as jnp
from jax import lax
from jax.experimental import pallas as pl
from jax.experimental.pallas import tpu as pltpu
from jax.sharding import PartitionSpec as P

LEVELS, ROWS, COLS = 4, 4, 9
TOK = LEVELS * ROWS * COLS
HEAD = 64
LANES = 128
CHUNK = 8 * TOK
EPSILON = 1e-05
NEG = -1e30
LOW = -3e38
MESH = pl.DeviceIdType.MESH
F32, BF16 = jnp.float32, jnp.bfloat16

SIDES = (
    (-1, 0, 0, 48),
    (1, 0, 48, 48),
    (0, -1, 96, 16),
    (0, 1, 112, 16),
    (-1, -1, 128, 16),
    (-1, 1, 144, 16),
    (1, -1, 160, 16),
    (1, 1, 176, 16),
)
OPPOSITE = (1, 0, 3, 2, 7, 6, 5, 4)
HALO_ROWS = 192


def cells_of(a, b):
    rows = {-1: [1], 1: [ROWS], 0: list(range(1, ROWS + 1))}[a]
    cols = {-1: [1], 1: [COLS], 0: list(range(1, COLS + 1))}[b]
    rim = [(r, c) for r in rows for c in cols]
    return rim, [(r + a, c + b) for r, c in rim]


def kernel(
    nlat, nz, ny,
    fields, conv_a, conv_b, key_list, key_count, w_qkv, w_out,
    att_out, mix_out,
    wq, wo, flat, grid, stream, stage, halo_f, halo_send, halo_recv,
    q_send, q_recv, kv_send, kv, near, qx, kt, vx, kn, vn, acc, top,
    s_even, s_odd, p_even, p_odd, f_even, f_odd, back_send, back_recv,
    w_sem, hs_sem, hr_sem, qs_sem, qr_sem, zs_sem, zr_sem, ys_sem, yr_sem, rs_sem, rr_sem, ls_sem, lr_sem, bs_sem, br_sem,
):
    lat = lax.axis_index("lat")
    lon = lax.axis_index("lon")
    z = lon // ny
    y = lon % ny
    nlon = nz * ny
    width = nz * LANES
    has_north = lat > 0
    has_south = lat < nlat - 1

    def wrap(i, n):
        return lax.rem(i + n, n)

    def at(zz, yy):
        return (lat, zz * ny + yy)

    wq_copy = pltpu.make_async_copy(w_qkv, wq, w_sem.at[0])
    wo_copy = pltpu.make_async_copy(w_out, wo, w_sem.at[1])
    wq_copy.start()
    wo_copy.start()

    barrier = pltpu.get_barrier_semaphore()

    def greet(dev):
        pl.semaphore_signal(barrier, inc=1, device_id=dev, device_id_type=MESH)

    for k in range(1, nz):
        greet(at(wrap(z + k, nz), y))
    greet(at(z, wrap(y + 1, ny)))
    greet(at(z, wrap(y - 1, ny)))
    greet((lat, wrap(lon + 1, nlon)))
    greet((lat, wrap(lon - 1, nlon)))

    @pl.when(has_north)
    def _():
        for d in (-1, 0, 1):
            greet((lat - 1, wrap(lon + d, nlon)))

    @pl.when(has_south)
    def _():
        for d in (-1, 0, 1):
            greet((lat + 1, wrap(lon + d, nlon)))

    for l in range(LEVELS):
        for c in range(COLS):
            cells = fields[l, c].astype(F32)
            for t in range(nz):
                flat[t, pl.ds((l * COLS + c) * ROWS, ROWS), :] = cells[:, t * LANES : (t + 1) * LANES]
    for r in range(ROWS):
        for c in range(COLS):
            for t in range(nz):
                grid[r + 1, c + 1, 0:LEVELS, t * LANES : (t + 1) * LANES] = flat[
                    t, pl.ds(c * ROWS + r, LEVELS, stride=COLS * ROWS), :
                ]

    def exists(a):
        return {-1: has_north, 0: None, 1: has_south}[a]

    def maybe(cond, fn):
        if cond is None:
            fn()
        else:
            pl.when(cond)(fn)

    def halo_copy(which, i):
        a, b, first, rows = SIDES[i]
        first_there = SIDES[OPPOSITE[i]][2]
        return pltpu.make_async_remote_copy(
            src_ref=halo_send.at[which, pl.ds(first, rows)],
            dst_ref=halo_recv.at[which, pl.ds(first_there, rows)],
            send_sem=hs_sem.at[which, i],
            recv_sem=hr_sem.at[which, OPPOSITE[i]],
            device_id=(lat + a, wrap(lon + b, nlon)),
            device_id_type=MESH,
        )

    def halo_wait(which, i):
        a, b, first, rows = SIDES[i]
        return pltpu.make_async_remote_copy(
            src_ref=halo_send.at[which, pl.ds(first, rows)],
            dst_ref=halo_recv.at[which, pl.ds(first, rows)],
            send_sem=hs_sem.at[which, i],
            recv_sem=hr_sem.at[which, i],
            device_id=(lat + a, wrap(lon + b, nlon)),
            device_id_type=MESH,
        )

    def halo_start(which):
        for i, (a, b, first, rows) in enumerate(SIDES):
            rim, _ = cells_of(a, b)
            for n, (r, c) in enumerate(rim):
                halo_f[pl.ds(first + 4 * n, 4), :] = grid[r, c, 0:LEVELS, :]
            halo_send[which, pl.ds(first, rows), :] = halo_f[pl.ds(first, rows), :].astype(BF16)
            maybe(exists(a), lambda: halo_copy(which, i).start())

    def halo_end(which):
        for i, (a, b, first, rows) in enumerate(SIDES):
            maybe(exists(a), lambda: halo_wait(which, i).wait_recv())
            halo_f[pl.ds(first, rows), :] = halo_recv[which, pl.ds(first, rows), :].astype(F32)
            _, beyond = cells_of(a, b)
            for n, (r, c) in enumerate(beyond):
                value = halo_f[pl.ds(first + 4 * n, 4), :]
                if a != 0:
                    value = jnp.where(exists(a), value, 0.0)
                grid[r, c, 0:LEVELS, :] = value

    def conv(weights, dst):
        chunk = min(256, width)
        for first in range(0, width, chunk):
            lanes = slice(first, first + chunk)
            w = weights[:, lanes]
            for r in range(ROWS):
                total = grid[r + 1, 1 : COLS + 1, 0:LEVELS, lanes]
                for a in range(3):
                    for b in range(3):
                        total = total + w[3 * a + b][None, None, :] * grid[r + a, b : b + COLS, 0:LEVELS, lanes]
                total = total.astype(BF16).astype(F32)
                for c in range(COLS):
                    for t in range(chunk // LANES):
                        dst[first // LANES + t, pl.ds((r * COLS + c) * LEVELS, LEVELS), :] = total[
                            c, :, t * LANES : (t + 1) * LANES
                        ]

    greetings = nz - 1 + 4 + 3 * has_north.astype(jnp.int32) + 3 * has_south.astype(jnp.int32)
    halo_f[...] = jnp.zeros_like(halo_f)
    pl.semaphore_wait(barrier, greetings)
    halo_start(0)

    lane = lax.broadcasted_iota(jnp.int32, (16, LANES), 1)
    count = key_count[0, 0]
    seen = ((lane == nlon) & has_north) | ((lane == nlon + 1) & has_south)
    for s in range(nlon):
        seen = seen | (lane == jnp.where(s < count, key_list[0, 0, s], -1))
    bias = jnp.where(seen, 0.0, NEG).astype(BF16)
    for k in range(nz):
        q_send[k, pl.ds(TOK, 16), :] = bias

    lane_t = lax.broadcasted_iota(jnp.int32, (TOK, LANES), 1)
    ones = jnp.ones((CHUNK, LANES), BF16)
    for u in range(2):
        vx[u, :, LANES:] = ones
        vn[u, :, LANES:] = ones[: 2 * TOK]
        for side in range(2):
            kn[u, pl.ds(side * TOK, TOK), LANES:] = jnp.where(lane_t == nlon + side, 1.0, 0.0).astype(BF16)
    vx[1, :, 0:LANES] = jnp.zeros((CHUNK, LANES), BF16)
    p_odd[...] = jnp.zeros_like(p_odd)
    f_odd[...] = jnp.ones_like(f_odd)

    def clear(o, carry):
        top[o] = jnp.full((2 * TOK, LANES), LOW, F32)
        acc[o] = jnp.zeros((2 * TOK, 2 * LANES), F32)
        return carry

    lax.fori_loop(0, nz, clear, 0)

    @pl.when(jnp.logical_not(has_north))
    def _():
        near[0] = jnp.zeros(near.shape[1:], BF16)

    @pl.when(jnp.logical_not(has_south))
    def _():
        near[1] = jnp.zeros(near.shape[1:], BF16)

    halo_end(0)
    conv(conv_a, stream)

    def tokens(ref):
        return jnp.concatenate([ref[t] for t in range(nz)], axis=1)

    def keep(ref, value):
        for t in range(nz):
            ref[t] = value[:, t * LANES : (t + 1) * LANES]

    x = tokens(stream)
    normed = (x * lax.rsqrt(jnp.mean(x * x, axis=-1, keepdims=True) + EPSILON)).astype(BF16)

    def shift(o):
        odd = o % 2
        return odd * ((o + 1) // 2) + (1 - odd) * ((nz - o // 2) % nz)

    def remote(src, dst, send_sem, recv_sem, dev):
        return pltpu.make_async_remote_copy(
            src_ref=src, dst_ref=dst, send_sem=send_sem, recv_sem=recv_sem, device_id=dev, device_id_type=MESH
        )

    def q_copy(o):
        there = wrap(z + shift(o), nz)
        return remote(q_send.at[there], q_recv.at[o], qs_sem.at[o], qr_sem.at[o], at(there, y))

    def z_copy(o):
        there = wrap(z + shift(o), nz)
        return remote(kv_send.at[there], kv.at[4 * o], zs_sem.at[o], zr_sem.at[o], at(there, y))

    def y_copy(way, o):
        return remote(
            kv.at[4 * o], kv.at[4 * o + 1 + way], ys_sem.at[way, o], yr_sem.at[way, o],
            at(z, wrap(y + 1 - 2 * way, ny)),
        )

    def relay_copy(way, o):
        rows = pl.ds(way * TOK, TOK)
        return remote(
            kv.at[4 * o + 1 + way, rows], kv.at[4 * o + 3, rows], rs_sem.at[way, o], rr_sem.at[way, o],
            at(z, wrap(y + 1 - 2 * way, ny)),
        )

    def lat_copy(way, o):
        return remote(
            kv.at[4 * o], near.at[1 - way, o], ls_sem.at[way, o], lr_sem.at[1 - way, o], (lat - 1 + 2 * way, lon)
        )

    def lat_wait(side, o):
        return remote(kv.at[4 * o], near.at[side, o], ls_sem.at[side, o], lr_sem.at[side, o], (lat - 1 + 2 * side, lon))

    def back_copy(o):
        return remote(
            back_send.at[o], back_recv.at[z], bs_sem.at[o], br_sem.at[o], at(wrap(z - shift(o), nz), y)
        )

    def back_wait(o):
        there = wrap(z + shift(o), nz)
        return remote(back_send.at[o], back_recv.at[there], bs_sem.at[o], br_sem.at[o], at(there, y))

    def project(part, j):
        cols = pl.ds(pl.multiple_of(part * width + j * 256, 256), 256)
        return jnp.dot(normed, wq[:, cols], preferred_element_type=F32)

    scale = HEAD ** -0.5 * math.log2(math.e)
    wq_copy.wait()
    for j in range(nz // 2):
        res = (project(0, j) * scale).astype(BF16)
        q_send[2 * j, pl.ds(0, TOK), :] = res[:, :LANES]
        q_send[2 * j + 1, pl.ds(0, TOK), :] = res[:, LANES:]
    for o in range(1, nz):
        q_copy(o).start()
    for j in range(nz // 2):
        for part in range(2):
            res = project(1 + part, j).astype(BF16)
            kv_send[2 * j, pl.ds(part * TOK, TOK), :] = res[:, :LANES]
            kv_send[2 * j + 1, pl.ds(part * TOK, TOK), :] = res[:, LANES:]
    for o in range(1, nz):
        z_copy(o).start()
    q_recv[0] = q_send[z]
    kv[0] = kv_send[z]

    def forward(o):
        y_copy(0, o).start()
        y_copy(1, o).start()

        @pl.when(has_north)
        def _():
            lat_copy(0, o).start()

        @pl.when(has_south)
        def _():
            lat_copy(1, o).start()

    def relay(o):
        for way in range(2):
            y_copy(way, o).wait_recv()
            relay_copy(way, o).start()

    def relayed(o):
        for way in range(2):
            relay_copy(way, o).wait_recv()

    forward(0)

    def prepare(o, carry):
        @pl.when(o > 0)
        def _():
            q_copy(o).wait_recv()

        q = q_recv[o, pl.ds(0, TOK), :]
        b = jnp.concatenate([q_recv[o, pl.ds(TOK, 16), :]] * (TOK // 16), axis=0)
        zero = jnp.zeros_like(q)
        qx[o, pl.ds(0, TOK), 0:LANES] = jnp.where(lane_t < HEAD, q, zero)
        qx[o, pl.ds(TOK, TOK), 0:LANES] = jnp.where(lane_t < HEAD, zero, q)
        qx[o, pl.ds(0, TOK), LANES:] = b
        qx[o, pl.ds(TOK, TOK), LANES:] = b
        return carry

    def chunk_keys(c, slot):
        keys = jnp.concatenate([kv[8 * c + i, pl.ds(0, TOK), :] for i in range(8)], axis=0)
        kt[slot, 0:LANES, :] = keys.T
        column = lax.broadcasted_iota(jnp.int32, (LANES, CHUNK), 1)
        number = jnp.zeros((LANES, CHUNK), jnp.int32)
        for i in range(8):
            yy = (y, wrap(y - 1, ny), wrap(y + 1, ny), wrap(y + 2, ny))[i % 4]
            here = wrap(z - shift(2 * c + i // 4), nz) * ny + yy
            number = jnp.where(column >= i * TOK, here, number)
        row = lax.broadcasted_iota(jnp.int32, (LANES, CHUNK), 0)
        kt[slot, LANES:, :] = jnp.where(row == number, 1.0, 0.0).astype(BF16)
        for i in range(8):
            vx[slot, pl.ds(i * TOK, TOK), 0:LANES] = kv[8 * c + i, pl.ds(TOK, TOK), :]

    def soften(s, o):
        old = top[o]
        new = jnp.maximum(old, jnp.max(s, axis=1, keepdims=True))
        top[o] = new
        return jnp.exp2(s - new[:, :1]).astype(BF16), jnp.exp2(old - new)

    def gain(o, factor, p, values):
        pv = jnp.dot(p, values, preferred_element_type=F32)
        return acc[o] * jnp.concatenate([factor, factor], axis=1) + pv

    z_copy(1).wait_recv()
    forward(1)
    relay(0)
    lax.fori_loop(0, nz, prepare, 0)
    relay(1)
    relayed(0)
    relayed(1)
    chunk_keys(0, 0)
    chunks = nz // 2
    steps = chunks * nz
    s_even[...] = jnp.dot(qx[0], kt[0], preferred_element_type=F32)
    s_refs, p_refs, f_refs = (s_even, s_odd), (p_even, p_odd), (f_even, f_odd)

    def advance(c, h):
        def act(a, fn):
            pl.when((h == a * (nz // 2) // 4) & (c < chunks - 1))(fn)

        def first():
            z_copy(2 * c + 2).wait_recv()
            forward(2 * c + 2)

        def second():
            z_copy(2 * c + 3).wait_recv()
            forward(2 * c + 3)
            relay(2 * c + 2)

        def third():
            relay(2 * c + 3)

        def fourth():
            relayed(2 * c + 2)
            relayed(2 * c + 3)
            chunk_keys(c + 1, (c + 1) % 2)

        act(0, first)
        act(1, second)
        act(2, third)
        act(3, fourth)

    def pair(t2, carry):
        advance(t2 // (nz // 2), t2 % (nz // 2))
        for u in range(2):
            t = 2 * t2 + u
            s_refs[1 - u][...] = jnp.dot(qx[(t + 1) % nz], kt[((t + 1) // nz) % 2], preferred_element_type=F32)
            p, factor = soften(s_refs[u][...], t % nz)
            before = (t + nz - 1) % nz
            acc[before] = gain(before, f_refs[1 - u][...], p_refs[1 - u][...], vx[((t + nz - 1) // nz + 1) % 2])
            p_refs[u][...] = p
            f_refs[u][...] = factor
        return carry

    lax.fori_loop(0, steps // 2, pair, 0)
    acc[nz - 1] = gain(nz - 1, f_odd[...], p_odd[...], vx[(chunks - 1) % 2])

    def finish(i, carry):
        numbers = [nz - 1 - 2 * i, nz - 2 - 2 * i]
        for u, o in enumerate(numbers):
            for side, cond in ((0, has_north), (1, has_south)):

                @pl.when(cond)
                def _():
                    lat_wait(side, o).wait_recv()

        for u, o in enumerate(numbers):
            for side in range(2):
                rows = pl.ds(side * TOK, TOK)
                kn[u, rows, 0:LANES] = near[side, o, pl.ds(0, TOK), :]
                vn[u, rows, 0:LANES] = near[side, o, pl.ds(TOK, TOK), :]
        scores = [
            lax.dot_general(qx[o], kn[u], (((1,), (1,)), ((), ())), preferred_element_type=F32)
            for u, o in enumerate(numbers)
        ]
        soft = [soften(s, o) for s, o in zip(scores, numbers)]
        for u, o in enumerate(numbers):
            p, factor = soft[u]
            result = gain(o, factor, p, vn[u])
            result = result[:, :LANES] / result[:, LANES:]
            result = jnp.where(lane_t < HEAD, result[:TOK], result[TOK:]).astype(BF16)
            back_send[o] = result

        for u, o in enumerate(numbers):

            @pl.when(o > 0)
            def _():
                back_copy(o).start()

        return carry

    lax.fori_loop(0, nz // 2, finish, 0)
    back_recv[z] = back_send[0]
    for o in range(1, nz):
        back_wait(o).wait_recv()

    attended = jnp.concatenate([back_recv[k] for k in range(nz)], axis=1)
    wo_copy.wait()
    after = tokens(stream) + jnp.dot(attended, wo[...], preferred_element_type=F32)
    keep(stage, after.astype(BF16).astype(F32))
    for r in range(ROWS):
        for c in range(COLS):
            for t in range(nz):
                grid[r + 1, c + 1, 0:LEVELS, t * LANES : (t + 1) * LANES] = stage[
                    t, pl.ds((r * COLS + c) * LEVELS, LEVELS), :
                ]
    halo_start(1)
    keep(stage, attended.astype(F32))

    def leave(out):
        for l in range(LEVELS):
            for c in range(COLS):
                for t in range(nz):
                    out[l, c, :, t * LANES : (t + 1) * LANES] = stage[
                        t, pl.ds(c * LEVELS + l, ROWS, stride=COLS * LEVELS), :
                    ].astype(BF16)

    leave(att_out)
    halo_end(1)
    conv(conv_b, stage)
    leave(mix_out)

    for which in range(2):
        for i, (a, b, first, rows) in enumerate(SIDES):
            maybe(exists(a), lambda: halo_copy(which, i).wait_send())

    def sent(o, carry):
        @pl.when(o > 0)
        def _():
            q_copy(o).wait_send()
            z_copy(o).wait_send()
            back_copy(o).wait_send()

        for way in range(2):
            y_copy(way, o).wait_send()
            relay_copy(way, o).wait_send()

        @pl.when(has_north)
        def _():
            lat_copy(0, o).wait_send()

        @pl.when(has_south)
        def _():
            lat_copy(1, o).wait_send()

        return carry

    lax.fori_loop(0, nz, sent, 0)


def local(nlat, nz, ny, fields, conv_first, w_qkv, w_out, conv_second, key_list, key_count):
    width = fields.shape[-1]
    vmem = pl.BlockSpec(memory_space=pltpu.VMEM)
    smem = pl.BlockSpec(memory_space=pltpu.SMEM)
    hbm = pl.BlockSpec(memory_space=pl.ANY)
    dma = pltpu.SemaphoreType.DMA
    fields = fields.transpose(0, 2, 1, 3)
    out = jax.ShapeDtypeStruct(fields.shape, BF16)
    attended, mixed = pl.pallas_call(
        functools.partial(kernel, nlat, nz, ny),
        out_shape=(out, out),
        in_specs=[vmem, vmem, vmem, smem, smem, hbm, hbm],
        out_specs=(vmem, vmem),
        scratch_shapes=[
            pltpu.VMEM(w_qkv.shape, BF16),
            pltpu.VMEM(w_out.shape, BF16),
            pltpu.VMEM((nz, TOK, LANES), F32),
            pltpu.VMEM((ROWS + 2, COLS + 2, 8, width), F32),
            pltpu.VMEM((nz, TOK, LANES), F32),
            pltpu.VMEM((nz, TOK, LANES), F32),
            pltpu.VMEM((HALO_ROWS, width), F32),
            pltpu.VMEM((2, HALO_ROWS, width), BF16),
            pltpu.VMEM((2, HALO_ROWS, width), BF16),
            pltpu.VMEM((nz, TOK + 16, LANES), BF16),
            pltpu.VMEM((nz, TOK + 16, LANES), BF16),
            pltpu.VMEM((nz, 2 * TOK, LANES), BF16),
            pltpu.VMEM((4 * nz, 2 * TOK, LANES), BF16),
            pltpu.VMEM((2, nz, 2 * TOK, LANES), BF16),
            pltpu.VMEM((nz, 2 * TOK, 2 * LANES), BF16),
            pltpu.VMEM((2, 2 * LANES, CHUNK), BF16),
            pltpu.VMEM((2, CHUNK, 2 * LANES), BF16),
            pltpu.VMEM((2, 2 * TOK, 2 * LANES), BF16),
            pltpu.VMEM((2, 2 * TOK, 2 * LANES), BF16),
            pltpu.VMEM((nz, 2 * TOK, 2 * LANES), F32),
            pltpu.VMEM((nz, 2 * TOK, LANES), F32),
            pltpu.VMEM((2 * TOK, CHUNK), F32),
            pltpu.VMEM((2 * TOK, CHUNK), F32),
            pltpu.VMEM((2 * TOK, CHUNK), BF16),
            pltpu.VMEM((2 * TOK, CHUNK), BF16),
            pltpu.VMEM((2 * TOK, LANES), F32),
            pltpu.VMEM((2 * TOK, LANES), F32),
            pltpu.VMEM((nz, TOK, LANES), BF16),
            pltpu.VMEM((nz, TOK, LANES), BF16),
            dma((2,)),
            dma((2, 8)),
            dma((2, 8)),
            dma((nz,)),
            dma((nz,)),
            dma((nz,)),
            dma((nz,)),
            dma((2, nz)),
            dma((2, nz)),
            dma((2, nz)),
            dma((2, nz)),
            dma((2, nz)),
            dma((2, nz)),
            dma((nz,)),
            dma((nz,)),
        ],
        compiler_params=pltpu.CompilerParams(
            collective_id=0, has_side_effects=True, vmem_limit_bytes=56 * 1024 * 1024
        ),
        name="block",
    )(fields, conv_first, conv_second, key_list, key_count, w_qkv, w_out)
    return attended.transpose(0, 2, 1, 3), mixed.transpose(0, 2, 1, 3)


def solution(mesh):
    nlat, nlon = mesh.shape["lat"], mesh.shape["lon"]
    nz = 8
    return jax.shard_map(
        functools.partial(local, nlat, nz, nlon // nz),
        mesh=mesh,
        in_specs=(
            P(None, "lat", "lon", None),
            P(),
            P(),
            P(),
            P(),
            P("lat", "lon", None),
            P("lat", "lon"),
        ),
        out_specs=(P(None, "lat", "lon", None), P(None, "lat", "lon", None)),
        check_vma=False,
    )
```

```python
import functools
import math

import jax
import jax.numpy as jnp
from jax import lax
from jax.experimental import pallas as pl
from jax.experimental.pallas import tpu as pltpu
from jax.sharding import PartitionSpec as P

LEVELS, ROWS, COLS = 4, 4, 9
TOK = LEVELS * ROWS * COLS
HEAD = 64
LANES = 128
CHUNK = 8 * TOK
EPSILON = 1e-05
NEG = -1e30
LOW = -3e38
MESH = pl.DeviceIdType.MESH
F32, BF16 = jnp.float32, jnp.bfloat16

SIDES = (
    (-1, 0, 0, 48),
    (1, 0, 48, 48),
    (0, -1, 96, 16),
    (0, 1, 112, 16),
    (-1, -1, 128, 16),
    (-1, 1, 144, 16),
    (1, -1, 160, 16),
    (1, 1, 176, 16),
)
OPPOSITE = (1, 0, 3, 2, 7, 6, 5, 4)
HALO_ROWS = 192


def cells_of(a, b):
    rows = {-1: [1], 1: [ROWS], 0: list(range(1, ROWS + 1))}[a]
    cols = {-1: [1], 1: [COLS], 0: list(range(1, COLS + 1))}[b]
    rim = [(r, c) for r in rows for c in cols]
    return rim, [(r + a, c + b) for r, c in rim]


def kernel(
    nlat, nz, ny,
    fields, conv_a, conv_b, key_list, key_count, w_qkv, w_out,
    att_out, mix_out,
    wq, wo, flat, grid, stream, stage, halo_f, halo_send, halo_recv,
    q_send, q_recv, kv_send, kv, near, qx, kt, vx, kn, vn, acc, top,
    s_even, s_odd, p_even, p_odd, f_even, f_odd, back_send, back_recv,
    w_sem, hs_sem, hr_sem, qs_sem, qr_sem, zs_sem, zr_sem, ys_sem, yr_sem, rs_sem, rr_sem, ls_sem, lr_sem, bs_sem, br_sem,
):
    lat = lax.axis_index("lat")
    lon = lax.axis_index("lon")
    z = lon // ny
    y = lon % ny
    nlon = nz * ny
    width = nz * LANES
    has_north = lat > 0
    has_south = lat < nlat - 1

    def wrap(i, n):
        return lax.rem(i + n, n)

    def at(zz, yy):
        return (lat, zz * ny + yy)

    wq_copy = pltpu.make_async_copy(w_qkv, wq, w_sem.at[0])
    wo_copy = pltpu.make_async_copy(w_out, wo, w_sem.at[1])
    wq_copy.start()
    wo_copy.start()

    barrier = pltpu.get_barrier_semaphore()

    def greet(dev):
        pl.semaphore_signal(barrier, inc=1, device_id=dev, device_id_type=MESH)

    for k in range(1, nz):
        greet(at(wrap(z + k, nz), y))
    greet(at(z, wrap(y + 1, ny)))
    greet(at(z, wrap(y - 1, ny)))
    greet((lat, wrap(lon + 1, nlon)))
    greet((lat, wrap(lon - 1, nlon)))

    @pl.when(has_north)
    def _():
        for d in (-1, 0, 1):
            greet((lat - 1, wrap(lon + d, nlon)))

    @pl.when(has_south)
    def _():
        for d in (-1, 0, 1):
            greet((lat + 1, wrap(lon + d, nlon)))

    for l in range(LEVELS):
        for c in range(COLS):
            cells = fields[l, c].astype(F32)
            for t in range(nz):
                flat[t, pl.ds((l * COLS + c) * ROWS, ROWS), :] = cells[:, t * LANES : (t + 1) * LANES]
    for r in range(ROWS):
        for c in range(COLS):
            for t in range(nz):
                grid[r + 1, c + 1, 0:LEVELS, t * LANES : (t + 1) * LANES] = flat[
                    t, pl.ds(c * ROWS + r, LEVELS, stride=COLS * ROWS), :
                ]

    def exists(a):
        return {-1: has_north, 0: None, 1: has_south}[a]

    def maybe(cond, fn):
        if cond is None:
            fn()
        else:
            pl.when(cond)(fn)

    def halo_copy(which, i):
        a, b, first, rows = SIDES[i]
        first_there = SIDES[OPPOSITE[i]][2]
        return pltpu.make_async_remote_copy(
            src_ref=halo_send.at[which, pl.ds(first, rows)],
            dst_ref=halo_recv.at[which, pl.ds(first_there, rows)],
            send_sem=hs_sem.at[which, i],
            recv_sem=hr_sem.at[which, OPPOSITE[i]],
            device_id=(lat + a, wrap(lon + b, nlon)),
            device_id_type=MESH,
        )

    def halo_wait(which, i):
        a, b, first, rows = SIDES[i]
        return pltpu.make_async_remote_copy(
            src_ref=halo_send.at[which, pl.ds(first, rows)],
            dst_ref=halo_recv.at[which, pl.ds(first, rows)],
            send_sem=hs_sem.at[which, i],
            recv_sem=hr_sem.at[which, i],
            device_id=(lat + a, wrap(lon + b, nlon)),
            device_id_type=MESH,
        )

    def halo_start(which):
        for i, (a, b, first, rows) in enumerate(SIDES):
            rim, _ = cells_of(a, b)
            for n, (r, c) in enumerate(rim):
                halo_f[pl.ds(first + 4 * n, 4), :] = grid[r, c, 0:LEVELS, :]
            halo_send[which, pl.ds(first, rows), :] = halo_f[pl.ds(first, rows), :].astype(BF16)
            maybe(exists(a), lambda: halo_copy(which, i).start())

    def halo_end(which):
        for i, (a, b, first, rows) in enumerate(SIDES):
            maybe(exists(a), lambda: halo_wait(which, i).wait_recv())
            halo_f[pl.ds(first, rows), :] = halo_recv[which, pl.ds(first, rows), :].astype(F32)
            _, beyond = cells_of(a, b)
            for n, (r, c) in enumerate(beyond):
                value = halo_f[pl.ds(first + 4 * n, 4), :]
                if a != 0:
                    value = jnp.where(exists(a), value, 0.0)
                grid[r, c, 0:LEVELS, :] = value

    def conv(weights, dst):
        chunk = min(256, width)
        for first in range(0, width, chunk):
            lanes = slice(first, first + chunk)
            w = weights[:, lanes]
            for r in range(ROWS):
                total = grid[r + 1, 1 : COLS + 1, 0:LEVELS, lanes]
                for a in range(3):
                    for b in range(3):
                        total = total + w[3 * a + b][None, None, :] * grid[r + a, b : b + COLS, 0:LEVELS, lanes]
                total = total.astype(BF16).astype(F32)
                for c in range(COLS):
                    for t in range(chunk // LANES):
                        dst[first // LANES + t, pl.ds((r * COLS + c) * LEVELS, LEVELS), :] = total[
                            c, :, t * LANES : (t + 1) * LANES
                        ]

    greetings = nz - 1 + 4 + 3 * has_north.astype(jnp.int32) + 3 * has_south.astype(jnp.int32)
    halo_f[...] = jnp.zeros_like(halo_f)
    pl.semaphore_wait(barrier, greetings)
    halo_start(0)

    lane = lax.broadcasted_iota(jnp.int32, (16, LANES), 1)
    count = key_count[0, 0]
    seen = ((lane == nlon) & has_north) | ((lane == nlon + 1) & has_south)
    for s in range(nlon):
        seen = seen | (lane == jnp.where(s < count, key_list[0, 0, s], -1))
    bias = jnp.where(seen, 0.0, NEG).astype(BF16)
    for k in range(nz):
        q_send[k, pl.ds(TOK, 16), :] = bias

    lane_t = lax.broadcasted_iota(jnp.int32, (TOK, LANES), 1)
    ones = jnp.ones((CHUNK, LANES), BF16)
    for u in range(2):
        vx[u, :, LANES:] = ones
        vn[u, :, LANES:] = ones[: 2 * TOK]
        for side in range(2):
            kn[u, pl.ds(side * TOK, TOK), LANES:] = jnp.where(lane_t == nlon + side, 1.0, 0.0).astype(BF16)
    vx[1, :, 0:LANES] = jnp.zeros((CHUNK, LANES), BF16)
    p_odd[...] = jnp.zeros_like(p_odd)
    f_odd[...] = jnp.ones_like(f_odd)

    def clear(o, carry):
        top[o] = jnp.full((2 * TOK, LANES), LOW, F32)
        acc[o] = jnp.zeros((2 * TOK, 2 * LANES), F32)
        return carry

    lax.fori_loop(0, nz, clear, 0)

    @pl.when(jnp.logical_not(has_north))
    def _():
        near[0] = jnp.zeros(near.shape[1:], BF16)

    @pl.when(jnp.logical_not(has_south))
    def _():
        near[1] = jnp.zeros(near.shape[1:], BF16)

    halo_end(0)
    conv(conv_a, stream)

    def tokens(ref):
        return jnp.concatenate([ref[t] for t in range(nz)], axis=1)

    def keep(ref, value):
        for t in range(nz):
            ref[t] = value[:, t * LANES : (t + 1) * LANES]

    x = tokens(stream)
    normed = (x * lax.rsqrt(jnp.mean(x * x, axis=-1, keepdims=True) + EPSILON)).astype(BF16)

    def shift(o):
        odd = o % 2
        return odd * ((o + 1) // 2) + (1 - odd) * ((nz - o // 2) % nz)

    def remote(src, dst, send_sem, recv_sem, dev):
        return pltpu.make_async_remote_copy(
            src_ref=src, dst_ref=dst, send_sem=send_sem, recv_sem=recv_sem, device_id=dev, device_id_type=MESH
        )

    def q_copy(o):
        there = wrap(z + shift(o), nz)
        return remote(q_send.at[there], q_recv.at[o], qs_sem.at[o], qr_sem.at[o], at(there, y))

    def z_copy(o):
        there = wrap(z + shift(o), nz)
        return remote(kv_send.at[there], kv.at[4 * o], zs_sem.at[o], zr_sem.at[o], at(there, y))

    def y_copy(way, o):
        return remote(
            kv.at[4 * o], kv.at[4 * o + 1 + way], ys_sem.at[way, o], yr_sem.at[way, o],
            at(z, wrap(y + 1 - 2 * way, ny)),
        )

    def relay_copy(way, o):
        rows = pl.ds(way * TOK, TOK)
        return remote(
            kv.at[4 * o + 1 + way, rows], kv.at[4 * o + 3, rows], rs_sem.at[way, o], rr_sem.at[way, o],
            at(z, wrap(y + 1 - 2 * way, ny)),
        )

    def lat_copy(way, o):
        return remote(
            kv.at[4 * o], near.at[1 - way, o], ls_sem.at[way, o], lr_sem.at[1 - way, o], (lat - 1 + 2 * way, lon)
        )

    def lat_wait(side, o):
        return remote(kv.at[4 * o], near.at[side, o], ls_sem.at[side, o], lr_sem.at[side, o], (lat - 1 + 2 * side, lon))

    def back_copy(o):
        return remote(
            back_send.at[o], back_recv.at[z], bs_sem.at[o], br_sem.at[o], at(wrap(z - shift(o), nz), y)
        )

    def back_wait(o):
        there = wrap(z + shift(o), nz)
        return remote(back_send.at[o], back_recv.at[there], bs_sem.at[o], br_sem.at[o], at(there, y))

    def project(part, j):
        cols = pl.ds(pl.multiple_of(part * width + j * 256, 256), 256)
        return jnp.dot(normed, wq[:, cols], preferred_element_type=F32)

    scale = HEAD ** -0.5 * math.log2(math.e)
    wq_copy.wait()
    for j in range(nz // 2):
        for part in range(2):
            res = project(1 + part, j).astype(BF16)
            kv_send[2 * j, pl.ds(part * TOK, TOK), :] = res[:, :LANES]
            kv_send[2 * j + 1, pl.ds(part * TOK, TOK), :] = res[:, LANES:]
    for o in range(1, 5):
        z_copy(o).start()
    kv[0] = kv_send[z]

    def forward(o):
        y_copy(0, o).start()
        y_copy(1, o).start()

        @pl.when(has_north)
        def _():
            lat_copy(0, o).start()

        @pl.when(has_south)
        def _():
            lat_copy(1, o).start()

    def relay(o):
        for way in range(2):
            y_copy(way, o).wait_recv()
            relay_copy(way, o).start()

    def relayed(o):
        for way in range(2):
            relay_copy(way, o).wait_recv()

    def arrive(o):
        z_copy(o).wait_recv()
        forward(o)
        if o + 4 < nz:
            z_copy(o + 4).start()

    forward(0)
    for j in range(nz // 2):
        res = (project(0, j) * scale).astype(BF16)
        q_send[2 * j, pl.ds(0, TOK), :] = res[:, :LANES]
        q_send[2 * j + 1, pl.ds(0, TOK), :] = res[:, LANES:]
    for o in range(1, nz):
        q_copy(o).start()
    q_recv[0] = q_send[z]

    def prepare(o, carry):
        @pl.when(o > 0)
        def _():
            q_copy(o).wait_recv()

        q = q_recv[o, pl.ds(0, TOK), :]
        b = jnp.concatenate([q_recv[o, pl.ds(TOK, 16), :]] * (TOK // 16), axis=0)
        zero = jnp.zeros_like(q)
        qx[o, pl.ds(0, TOK), 0:LANES] = jnp.where(lane_t < HEAD, q, zero)
        qx[o, pl.ds(TOK, TOK), 0:LANES] = jnp.where(lane_t < HEAD, zero, q)
        qx[o, pl.ds(0, TOK), LANES:] = b
        qx[o, pl.ds(TOK, TOK), LANES:] = b
        return carry

    def chunk_keys(c, slot):
        keys = jnp.concatenate([kv[8 * c + i, pl.ds(0, TOK), :] for i in range(8)], axis=0)
        kt[slot, 0:LANES, :] = keys.T
        column = lax.broadcasted_iota(jnp.int32, (LANES, CHUNK), 1)
        number = jnp.zeros((LANES, CHUNK), jnp.int32)
        for i in range(8):
            yy = (y, wrap(y - 1, ny), wrap(y + 1, ny), wrap(y + 2, ny))[i % 4]
            here = wrap(z - shift(2 * c + i // 4), nz) * ny + yy
            number = jnp.where(column >= i * TOK, here, number)
        row = lax.broadcasted_iota(jnp.int32, (LANES, CHUNK), 0)
        kt[slot, LANES:, :] = jnp.where(row == number, 1.0, 0.0).astype(BF16)
        for i in range(8):
            vx[slot, pl.ds(i * TOK, TOK), 0:LANES] = kv[8 * c + i, pl.ds(TOK, TOK), :]

    def soften(s, o):
        old = top[o]
        new = jnp.maximum(old, jnp.max(s, axis=1, keepdims=True))
        top[o] = new
        return jnp.exp2(s - new[:, :1]).astype(BF16), jnp.exp2(old - new)

    def gain(o, factor, p, values):
        pv = jnp.dot(p, values, preferred_element_type=F32)
        return acc[o] * jnp.concatenate([factor, factor], axis=1) + pv

    chunks = nz // 2
    steps = chunks * nz
    half = nz // 2
    arrive(1)
    relay(0)
    arrive(2)
    relay(1)
    prepare(0, 0)
    relayed(0)
    relayed(1)
    chunk_keys(0, 0)
    if nz > 4:
        plan = {
            0: [(arrive, 3), (relay, 2)],
            1: [(arrive, 4), (relay, 3)],
            2: [(arrive, 5)],
            3: [(relay, 4)],
            4: [(arrive, 6), (relay, 5)],
            5: [(arrive, 7)],
            6: [(relay, 6)],
            8: [(relay, 7)],
        }
        late = []
    else:
        plan = {}
        late = [(relay, 2), (arrive, 3), (relay, 3)]
    s_refs, p_refs, f_refs = (s_even, s_odd), (p_even, p_odd), (f_even, f_odd)

    def advance(t2):
        for when, acts in plan.items():

            @pl.when(t2 == when)
            def _():
                for fn, o in acts:
                    fn(o)

        c = t2 // half

        @pl.when((t2 % half == half - 1) & (c < chunks - 2))
        def _():
            relayed(2 * c + 2)
            relayed(2 * c + 3)
            chunk_keys(c + 1, (c + 1) % 2)

    def pair(t2, carry):
        for i in (1, 2):

            @pl.when(2 * t2 + i < nz)
            def _():
                prepare(2 * t2 + i, 0)

        advance(t2)
        for u in range(2):
            t = 2 * t2 + u
            s_refs[1 - u][...] = jnp.dot(qx[(t + 1) % nz], kt[((t + 1) // nz) % 2], preferred_element_type=F32)
            p, factor = soften(s_refs[u][...], t % nz)
            before = (t + nz - 1) % nz
            acc[before] = gain(before, f_refs[1 - u][...], p_refs[1 - u][...], vx[((t + nz - 1) // nz + 1) % 2])
            p_refs[u][...] = p
            f_refs[u][...] = factor
        return carry

    s_even[...] = jnp.dot(qx[0], kt[0], preferred_element_type=F32)
    lax.fori_loop(0, (chunks - 1) * half, pair, 0)
    acc[nz - 1] = gain(nz - 1, f_odd[...], p_odd[...], vx[(chunks - 2) % 2])
    last = chunks - 1
    for fn, o in late:
        fn(o)

    def beside(i, carry):
        numbers = [2 * i, 2 * i + 1]
        for u, o in enumerate(numbers):
            for side, cond in ((0, has_north), (1, has_south)):

                @pl.when(cond)
                def _():
                    lat_wait(side, o).wait_recv()

        for u, o in enumerate(numbers):
            for side in range(2):
                rows = pl.ds(side * TOK, TOK)
                kn[u, rows, 0:LANES] = near[side, o, pl.ds(0, TOK), :]
                vn[u, rows, 0:LANES] = near[side, o, pl.ds(TOK, TOK), :]
        scores = [
            lax.dot_general(qx[o], kn[u], (((1,), (1,)), ((), ())), preferred_element_type=F32)
            for u, o in enumerate(numbers)
        ]
        soft = [soften(s, o) for s, o in zip(scores, numbers)]
        for u, o in enumerate(numbers):
            p, factor = soft[u]
            acc[o] = gain(o, factor, p, vn[u])
        return carry

    lax.fori_loop(0, nz // 2, beside, 0)

    relayed(2 * last)
    relayed(2 * last + 1)
    chunk_keys(last, last % 2)
    keys_last, values_last = kt.at[last % 2], vx.at[last % 2]
    p_odd[...] = jnp.zeros_like(p_odd)
    f_odd[...] = jnp.ones_like(f_odd)

    def result(o, factor, p):
        total = gain(o, factor, p, values_last[...])
        total = total[:, :LANES] / total[:, LANES:]
        return jnp.where(lane_t < HEAD, total[:TOK], total[TOK:]).astype(BF16)

    def finish(i2, carry):
        for u in range(2):
            i = 2 * i2 + u
            o = nz - 1 - i
            s_refs[1 - u][...] = jnp.dot(qx[(o + nz - 1) % nz], keys_last[...], preferred_element_type=F32)
            p, factor = soften(s_refs[u][...], o)
            before = (o + 1) % nz
            back_send[before] = result(before, f_refs[1 - u][...], p_refs[1 - u][...])
            p_refs[u][...] = p
            f_refs[u][...] = factor

            @pl.when(i > 0)
            def _():
                back_copy(before).start()

        return carry

    s_even[...] = jnp.dot(qx[nz - 1], keys_last[...], preferred_element_type=F32)
    lax.fori_loop(0, half, finish, 0)
    back_recv[z] = result(0, f_odd[...], p_odd[...])
    for o in range(1, nz):
        back_wait(o).wait_recv()

    attended = jnp.concatenate([back_recv[k] for k in range(nz)], axis=1)
    wo_copy.wait()
    after = tokens(stream) + jnp.dot(attended, wo[...], preferred_element_type=F32)
    keep(stage, after.astype(BF16).astype(F32))
    for r in range(ROWS):
        for c in range(COLS):
            for t in range(nz):
                grid[r + 1, c + 1, 0:LEVELS, t * LANES : (t + 1) * LANES] = stage[
                    t, pl.ds((r * COLS + c) * LEVELS, LEVELS), :
                ]
    halo_start(1)
    keep(stage, attended.astype(F32))

    def leave(out):
        for l in range(LEVELS):
            for c in range(COLS):
                for t in range(nz):
                    out[l, c, :, t * LANES : (t + 1) * LANES] = stage[
                        t, pl.ds(c * LEVELS + l, ROWS, stride=COLS * LEVELS), :
                    ].astype(BF16)

    leave(att_out)
    halo_end(1)
    conv(conv_b, stage)
    leave(mix_out)

    for which in range(2):
        for i, (a, b, first, rows) in enumerate(SIDES):
            maybe(exists(a), lambda: halo_copy(which, i).wait_send())

    def sent(o, carry):
        @pl.when(o > 0)
        def _():
            q_copy(o).wait_send()
            z_copy(o).wait_send()
            back_copy(o).wait_send()

        for way in range(2):
            y_copy(way, o).wait_send()
            relay_copy(way, o).wait_send()

        @pl.when(has_north)
        def _():
            lat_copy(0, o).wait_send()

        @pl.when(has_south)
        def _():
            lat_copy(1, o).wait_send()

        return carry

    lax.fori_loop(0, nz, sent, 0)


def local(nlat, nz, ny, fields, conv_first, w_qkv, w_out, conv_second, key_list, key_count):
    width = fields.shape[-1]
    vmem = pl.BlockSpec(memory_space=pltpu.VMEM)
    smem = pl.BlockSpec(memory_space=pltpu.SMEM)
    hbm = pl.BlockSpec(memory_space=pl.ANY)
    dma = pltpu.SemaphoreType.DMA
    fields = fields.transpose(0, 2, 1, 3)
    out = jax.ShapeDtypeStruct(fields.shape, BF16)
    attended, mixed = pl.pallas_call(
        functools.partial(kernel, nlat, nz, ny),
        out_shape=(out, out),
        in_specs=[vmem, vmem, vmem, smem, smem, hbm, hbm],
        out_specs=(vmem, vmem),
        scratch_shapes=[
            pltpu.VMEM(w_qkv.shape, BF16),
            pltpu.VMEM(w_out.shape, BF16),
            pltpu.VMEM((nz, TOK, LANES), F32),
            pltpu.VMEM((ROWS + 2, COLS + 2, 8, width), F32),
            pltpu.VMEM((nz, TOK, LANES), F32),
            pltpu.VMEM((nz, TOK, LANES), F32),
            pltpu.VMEM((HALO_ROWS, width), F32),
            pltpu.VMEM((2, HALO_ROWS, width), BF16),
            pltpu.VMEM((2, HALO_ROWS, width), BF16),
            pltpu.VMEM((nz, TOK + 16, LANES), BF16),
            pltpu.VMEM((nz, TOK + 16, LANES), BF16),
            pltpu.VMEM((nz, 2 * TOK, LANES), BF16),
            pltpu.VMEM((4 * nz, 2 * TOK, LANES), BF16),
            pltpu.VMEM((2, nz, 2 * TOK, LANES), BF16),
            pltpu.VMEM((nz, 2 * TOK, 2 * LANES), BF16),
            pltpu.VMEM((2, 2 * LANES, CHUNK), BF16),
            pltpu.VMEM((2, CHUNK, 2 * LANES), BF16),
            pltpu.VMEM((2, 2 * TOK, 2 * LANES), BF16),
            pltpu.VMEM((2, 2 * TOK, 2 * LANES), BF16),
            pltpu.VMEM((nz, 2 * TOK, 2 * LANES), F32),
            pltpu.VMEM((nz, 2 * TOK, LANES), F32),
            pltpu.VMEM((2 * TOK, CHUNK), F32),
            pltpu.VMEM((2 * TOK, CHUNK), F32),
            pltpu.VMEM((2 * TOK, CHUNK), BF16),
            pltpu.VMEM((2 * TOK, CHUNK), BF16),
            pltpu.VMEM((2 * TOK, LANES), F32),
            pltpu.VMEM((2 * TOK, LANES), F32),
            pltpu.VMEM((nz, TOK, LANES), BF16),
            pltpu.VMEM((nz, TOK, LANES), BF16),
            dma((2,)),
            dma((2, 8)),
            dma((2, 8)),
            dma((nz,)),
            dma((nz,)),
            dma((nz,)),
            dma((nz,)),
            dma((2, nz)),
            dma((2, nz)),
            dma((2, nz)),
            dma((2, nz)),
            dma((2, nz)),
            dma((2, nz)),
            dma((nz,)),
            dma((nz,)),
        ],
        compiler_params=pltpu.CompilerParams(
            collective_id=0, has_side_effects=True, vmem_limit_bytes=56 * 1024 * 1024
        ),
        name="block",
    )(fields, conv_first, conv_second, key_list, key_count, w_qkv, w_out)
    return attended.transpose(0, 2, 1, 3), mixed.transpose(0, 2, 1, 3)


def solution(mesh):
    nlat, nlon = mesh.shape["lat"], mesh.shape["lon"]
    nz = 8
    return jax.shard_map(
        functools.partial(local, nlat, nz, nlon // nz),
        mesh=mesh,
        in_specs=(
            P(None, "lat", "lon", None),
            P(),
            P(),
            P(),
            P(),
            P("lat", "lon", None),
            P("lat", "lon"),
        ),
        out_specs=(P(None, "lat", "lon", None), P(None, "lat", "lon", None)),
        check_vma=False,
    )
```

```python
import functools
import math

import jax
import jax.numpy as jnp
from jax import lax
from jax.experimental import pallas as pl
from jax.experimental.pallas import tpu as pltpu
from jax.sharding import PartitionSpec as P

LEVELS, ROWS, COLS = 4, 4, 9
TOK = LEVELS * ROWS * COLS
HEAD = 64
LANES = 128
CHUNK = 8 * TOK
MARKS = 48
EPSILON = 1e-05
NEG = -1e30
LOW = -3e38
MESH = pl.DeviceIdType.MESH
F32, BF16 = jnp.float32, jnp.bfloat16

SIDES = (
    (-1, 0, 0, 48),
    (1, 0, 48, 48),
    (0, -1, 96, 16),
    (0, 1, 112, 16),
    (-1, -1, 128, 16),
    (-1, 1, 144, 16),
    (1, -1, 160, 16),
    (1, 1, 176, 16),
)
OPPOSITE = (1, 0, 3, 2, 7, 6, 5, 4)
HALO_ROWS = 192


def cells_of(a, b):
    rows = {-1: [1], 1: [ROWS], 0: list(range(1, ROWS + 1))}[a]
    cols = {-1: [1], 1: [COLS], 0: list(range(1, COLS + 1))}[b]
    rim = [(r, c) for r in rows for c in cols]
    return rim, [(r + a, c + b) for r, c in rim]


def kernel(
    nlat, nz, ny,
    fields, conv_a, conv_b, key_list, key_count, w_qkv, w_out,
    att_out, mix_out,
    wq, wo, flat, grid, stream, stage, halo_f, halo_send, halo_recv,
    q_send, q_recv, kv_send, kv, near, qx, kt, vx, kn, vn, acc, top,
    s_even, s_odd, p_even, p_odd, f_even, f_odd, back_send, back_recv,
    w_sem, hs_sem, hr_sem, qs_sem, qr_sem, zs_sem, zr_sem, ys_sem, yr_sem, rs_sem, rr_sem, ls_sem, lr_sem, bs_sem, br_sem,
):
    lat = lax.axis_index("lat")
    lon = lax.axis_index("lon")
    z = lon // ny
    y = lon % ny
    nlon = nz * ny
    width = nz * LANES
    has_north = lat > 0
    has_south = lat < nlat - 1

    def wrap(i, n):
        return lax.rem(i + n, n)

    def at(zz, yy):
        return (lat, zz * ny + yy)

    wq_copy = pltpu.make_async_copy(w_qkv, wq, w_sem.at[0])
    wo_copy = pltpu.make_async_copy(w_out, wo, w_sem.at[1])
    wq_copy.start()
    wo_copy.start()

    barrier = pltpu.get_barrier_semaphore()

    def greet(dev):
        pl.semaphore_signal(barrier, inc=1, device_id=dev, device_id_type=MESH)

    for k in range(1, nz):
        greet(at(wrap(z + k, nz), y))
    greet(at(z, wrap(y + 1, ny)))
    greet(at(z, wrap(y - 1, ny)))
    greet((lat, wrap(lon + 1, nlon)))
    greet((lat, wrap(lon - 1, nlon)))

    @pl.when(has_north)
    def _():
        for d in (-1, 0, 1):
            greet((lat - 1, wrap(lon + d, nlon)))

    @pl.when(has_south)
    def _():
        for d in (-1, 0, 1):
            greet((lat + 1, wrap(lon + d, nlon)))

    for l in range(LEVELS):
        for c in range(COLS):
            cells = fields[l, c].astype(F32)
            for t in range(nz):
                flat[t, pl.ds((l * COLS + c) * ROWS, ROWS), :] = cells[:, t * LANES : (t + 1) * LANES]
    for r in range(ROWS):
        for c in range(COLS):
            for t in range(nz):
                grid[r + 1, c + 1, 0:LEVELS, t * LANES : (t + 1) * LANES] = flat[
                    t, pl.ds(c * ROWS + r, LEVELS, stride=COLS * ROWS), :
                ]

    def exists(a):
        return {-1: has_north, 0: None, 1: has_south}[a]

    def maybe(cond, fn):
        if cond is None:
            fn()
        else:
            pl.when(cond)(fn)

    def halo_copy(which, i):
        a, b, first, rows = SIDES[i]
        first_there = SIDES[OPPOSITE[i]][2]
        return pltpu.make_async_remote_copy(
            src_ref=halo_send.at[which, pl.ds(first, rows)],
            dst_ref=halo_recv.at[which, pl.ds(first_there, rows)],
            send_sem=hs_sem.at[which, i],
            recv_sem=hr_sem.at[which, OPPOSITE[i]],
            device_id=(lat + a, wrap(lon + b, nlon)),
            device_id_type=MESH,
        )

    def halo_wait(which, i):
        a, b, first, rows = SIDES[i]
        return pltpu.make_async_remote_copy(
            src_ref=halo_send.at[which, pl.ds(first, rows)],
            dst_ref=halo_recv.at[which, pl.ds(first, rows)],
            send_sem=hs_sem.at[which, i],
            recv_sem=hr_sem.at[which, i],
            device_id=(lat + a, wrap(lon + b, nlon)),
            device_id_type=MESH,
        )

    def halo_start(which):
        for i, (a, b, first, rows) in enumerate(SIDES):
            rim, _ = cells_of(a, b)
            for n, (r, c) in enumerate(rim):
                halo_f[pl.ds(first + 4 * n, 4), :] = grid[r, c, 0:LEVELS, :]
            halo_send[which, pl.ds(first, rows), :] = halo_f[pl.ds(first, rows), :].astype(BF16)
            maybe(exists(a), lambda: halo_copy(which, i).start())

    def halo_end(which):
        for i, (a, b, first, rows) in enumerate(SIDES):
            maybe(exists(a), lambda: halo_wait(which, i).wait_recv())
            halo_f[pl.ds(first, rows), :] = halo_recv[which, pl.ds(first, rows), :].astype(F32)
            _, beyond = cells_of(a, b)
            for n, (r, c) in enumerate(beyond):
                value = halo_f[pl.ds(first + 4 * n, 4), :]
                if a != 0:
                    value = jnp.where(exists(a), value, 0.0)
                grid[r, c, 0:LEVELS, :] = value

    def conv(weights, dst):
        chunk = min(256, width)
        for first in range(0, width, chunk):
            lanes = slice(first, first + chunk)
            w = weights[:, lanes]
            for r in range(ROWS):
                total = grid[r + 1, 1 : COLS + 1, 0:LEVELS, lanes]
                for a in range(3):
                    for b in range(3):
                        total = total + w[3 * a + b][None, None, :] * grid[r + a, b : b + COLS, 0:LEVELS, lanes]
                total = total.astype(BF16).astype(F32)
                for c in range(COLS):
                    for t in range(chunk // LANES):
                        dst[first // LANES + t, pl.ds((r * COLS + c) * LEVELS, LEVELS), :] = total[
                            c, :, t * LANES : (t + 1) * LANES
                        ]

    greetings = nz - 1 + 4 + 3 * has_north.astype(jnp.int32) + 3 * has_south.astype(jnp.int32)
    halo_f[...] = jnp.zeros_like(halo_f)
    pl.semaphore_wait(barrier, greetings)
    halo_start(0)

    lane = lax.broadcasted_iota(jnp.int32, (16, LANES), 1)
    count = key_count[0, 0]
    seen = ((lane == nlon) & has_north) | ((lane == nlon + 1) & has_south)
    for s in range(nlon):
        seen = seen | (lane == jnp.where(s < count, key_list[0, 0, s], -1))
    bias = jnp.where(seen, 0.0, NEG).astype(BF16)
    for k in range(nz):
        q_send[k, pl.ds(TOK, 16), :] = bias

    lane_t = lax.broadcasted_iota(jnp.int32, (TOK, LANES), 1)
    ones = jnp.ones((CHUNK, LANES), BF16)
    for u in range(2):
        kt[u, LANES + MARKS :, :] = jnp.zeros((LANES - MARKS, CHUNK), BF16)
        vx[u, :, LANES:] = ones
        vn[u, :, LANES:] = ones[: 2 * TOK]
        for side in range(2):
            kn[u, pl.ds(side * TOK, TOK), LANES:] = jnp.where(lane_t == nlon + side, 1.0, 0.0).astype(BF16)
    vx[1, :, 0:LANES] = jnp.zeros((CHUNK, LANES), BF16)
    p_odd[...] = jnp.zeros_like(p_odd)
    f_odd[...] = jnp.ones_like(f_odd)

    def clear(o, carry):
        top[o] = jnp.full((2 * TOK, LANES), LOW, F32)
        acc[o] = jnp.zeros((2 * TOK, 2 * LANES), F32)
        return carry

    lax.fori_loop(0, nz, clear, 0)

    @pl.when(jnp.logical_not(has_north))
    def _():
        near[0] = jnp.zeros(near.shape[1:], BF16)

    @pl.when(jnp.logical_not(has_south))
    def _():
        near[1] = jnp.zeros(near.shape[1:], BF16)

    halo_end(0)
    conv(conv_a, stream)

    def tokens(ref):
        return jnp.concatenate([ref[t] for t in range(nz)], axis=1)

    def keep(ref, value):
        for t in range(nz):
            ref[t] = value[:, t * LANES : (t + 1) * LANES]

    x = tokens(stream)
    normed = (x * lax.rsqrt(jnp.mean(x * x, axis=-1, keepdims=True) + EPSILON)).astype(BF16)

    def shift(o):
        odd = o % 2
        return odd * ((o + 1) // 2) + (1 - odd) * ((nz - o // 2) % nz)

    def remote(src, dst, send_sem, recv_sem, dev):
        return pltpu.make_async_remote_copy(
            src_ref=src, dst_ref=dst, send_sem=send_sem, recv_sem=recv_sem, device_id=dev, device_id_type=MESH
        )

    def q_copy(o):
        there = wrap(z + shift(o), nz)
        return remote(q_send.at[there], q_recv.at[o], qs_sem.at[o], qr_sem.at[o], at(there, y))

    def z_copy(o):
        there = wrap(z + shift(o), nz)
        return remote(kv_send.at[there], kv.at[4 * o], zs_sem.at[o], zr_sem.at[o], at(there, y))

    def y_copy(way, o):
        return remote(
            kv.at[4 * o], kv.at[4 * o + 1 + way], ys_sem.at[way, o], yr_sem.at[way, o],
            at(z, wrap(y + 1 - 2 * way, ny)),
        )

    def relay_copy(way, o):
        rows = pl.ds(way * TOK, TOK)
        return remote(
            kv.at[4 * o + 1 + way, rows], kv.at[4 * o + 3, rows], rs_sem.at[way, o], rr_sem.at[way, o],
            at(z, wrap(y + 1 - 2 * way, ny)),
        )

    def lat_copy(way, o):
        return remote(
            kv.at[4 * o], near.at[1 - way, o], ls_sem.at[way, o], lr_sem.at[1 - way, o], (lat - 1 + 2 * way, lon)
        )

    def lat_wait(side, o):
        return remote(kv.at[4 * o], near.at[side, o], ls_sem.at[side, o], lr_sem.at[side, o], (lat - 1 + 2 * side, lon))

    def back_copy(o):
        return remote(
            back_send.at[o], back_recv.at[z], bs_sem.at[o], br_sem.at[o], at(wrap(z - shift(o), nz), y)
        )

    def back_wait(o):
        there = wrap(z + shift(o), nz)
        return remote(back_send.at[o], back_recv.at[there], bs_sem.at[o], br_sem.at[o], at(there, y))

    def project(part, j):
        cols = pl.ds(pl.multiple_of(part * width + j * 256, 256), 256)
        return jnp.dot(normed, wq[:, cols], preferred_element_type=F32)

    scale = HEAD ** -0.5 * math.log2(math.e)
    wq_copy.wait()
    for j in range(nz // 2):
        for part in range(2):
            res = project(1 + part, j).astype(BF16)
            kv_send[2 * j, pl.ds(part * TOK, TOK), :] = res[:, :LANES]
            kv_send[2 * j + 1, pl.ds(part * TOK, TOK), :] = res[:, LANES:]
    for o in range(1, 5):
        z_copy(o).start()
    kv[0] = kv_send[z]

    def forward(o):
        y_copy(0, o).start()
        y_copy(1, o).start()

        @pl.when(has_north)
        def _():
            lat_copy(0, o).start()

        @pl.when(has_south)
        def _():
            lat_copy(1, o).start()

    def relay(o):
        for way in range(2):
            y_copy(way, o).wait_recv()
            relay_copy(way, o).start()

    def relayed(o):
        for way in range(2):
            relay_copy(way, o).wait_recv()

    def arrive(o):
        z_copy(o).wait_recv()
        forward(o)
        if o + 4 < nz:
            z_copy(o + 4).start()

    forward(0)
    for j in range(nz // 2):
        res = (project(0, j) * scale).astype(BF16)
        q_send[2 * j, pl.ds(0, TOK), :] = res[:, :LANES]
        q_send[2 * j + 1, pl.ds(0, TOK), :] = res[:, LANES:]
    for o in range(1, nz):
        q_copy(o).start()
    q_recv[0] = q_send[z]

    def prepare(o, carry):
        @pl.when(o > 0)
        def _():
            q_copy(o).wait_recv()

        q = q_recv[o, pl.ds(0, TOK), :]
        b = jnp.concatenate([q_recv[o, pl.ds(TOK, 16), :]] * (TOK // 16), axis=0)
        zero = jnp.zeros_like(q)
        qx[o, pl.ds(0, TOK), 0:LANES] = jnp.where(lane_t < HEAD, q, zero)
        qx[o, pl.ds(TOK, TOK), 0:LANES] = jnp.where(lane_t < HEAD, zero, q)
        qx[o, pl.ds(0, TOK), LANES:] = b
        qx[o, pl.ds(TOK, TOK), LANES:] = b
        return carry

    def chunk_keys(c, slot):
        keys = jnp.concatenate([kv[8 * c + i, pl.ds(0, TOK), :] for i in range(8)], axis=0)
        kt[slot, 0:LANES, :] = keys.T
        column = lax.broadcasted_iota(jnp.int32, (1, CHUNK), 1)
        number = jnp.zeros((1, CHUNK), jnp.int32)
        for i in range(8):
            yy = (y, wrap(y - 1, ny), wrap(y + 1, ny), wrap(y + 2, ny))[i % 4]
            here = wrap(z - shift(2 * c + i // 4), nz) * ny + yy
            number = jnp.where(column >= i * TOK, here, number)
        row = lax.broadcasted_iota(jnp.int32, (MARKS, CHUNK), 0)
        kt[slot, LANES : LANES + MARKS, :] = jnp.where(row == number, 1.0, 0.0).astype(BF16)
        for i in range(8):
            vx[slot, pl.ds(i * TOK, TOK), 0:LANES] = kv[8 * c + i, pl.ds(TOK, TOK), :]

    def soften(s, o):
        old = top[o]
        new = jnp.maximum(old, jnp.max(s, axis=1, keepdims=True))
        top[o] = new
        return jnp.exp2(s - new[:, :1]).astype(BF16), jnp.exp2(old - new)

    def gain(o, factor, p, values):
        pv = jnp.dot(p, values, preferred_element_type=F32)
        return acc[o] * jnp.concatenate([factor, factor], axis=1) + pv

    chunks = nz // 2
    steps = chunks * nz
    half = nz // 2
    arrive(1)
    relay(0)
    arrive(2)
    relay(1)
    prepare(0, 0)
    relayed(0)
    relayed(1)
    chunk_keys(0, 0)
    if nz > 4:
        plan = {
            0: [(arrive, 3), (relay, 2)],
            1: [(arrive, 4), (relay, 3)],
            2: [(arrive, 5)],
            3: [(relay, 4)],
            4: [(arrive, 6), (relay, 5)],
            5: [(arrive, 7)],
            6: [(relay, 6)],
            8: [(relay, 7)],
        }
        late = []
    else:
        plan = {}
        late = [(relay, 2), (arrive, 3), (relay, 3)]
    s_refs, p_refs, f_refs = (s_even, s_odd), (p_even, p_odd), (f_even, f_odd)

    def advance(t2):
        for when, acts in plan.items():

            @pl.when(t2 == when)
            def _():
                for fn, o in acts:
                    fn(o)

        c = t2 // half

        @pl.when((t2 % half == half - 1) & (c < chunks - 2))
        def _():
            relayed(2 * c + 2)
            relayed(2 * c + 3)
            chunk_keys(c + 1, (c + 1) % 2)

    def pair(t2, carry):
        for i in (1, 2):

            @pl.when(2 * t2 + i < nz)
            def _():
                prepare(2 * t2 + i, 0)

        advance(t2)
        for u in range(2):
            t = 2 * t2 + u
            s_refs[1 - u][...] = jnp.dot(qx[(t + 1) % nz], kt[((t + 1) // nz) % 2], preferred_element_type=F32)
            p, factor = soften(s_refs[u][...], t % nz)
            before = (t + nz - 1) % nz
            acc[before] = gain(before, f_refs[1 - u][...], p_refs[1 - u][...], vx[((t + nz - 1) // nz + 1) % 2])
            p_refs[u][...] = p
            f_refs[u][...] = factor
        return carry

    s_even[...] = jnp.dot(qx[0], kt[0], preferred_element_type=F32)
    lax.fori_loop(0, (chunks - 1) * half, pair, 0)
    acc[nz - 1] = gain(nz - 1, f_odd[...], p_odd[...], vx[(chunks - 2) % 2])
    last = chunks - 1
    for fn, o in late:
        fn(o)

    def beside(i, carry):
        numbers = [2 * i, 2 * i + 1]
        for u, o in enumerate(numbers):
            for side, cond in ((0, has_north), (1, has_south)):

                @pl.when(cond)
                def _():
                    lat_wait(side, o).wait_recv()

        for u, o in enumerate(numbers):
            for side in range(2):
                rows = pl.ds(side * TOK, TOK)
                kn[u, rows, 0:LANES] = near[side, o, pl.ds(0, TOK), :]
                vn[u, rows, 0:LANES] = near[side, o, pl.ds(TOK, TOK), :]
        scores = [
            lax.dot_general(qx[o], kn[u], (((1,), (1,)), ((), ())), preferred_element_type=F32)
            for u, o in enumerate(numbers)
        ]
        soft = [soften(s, o) for s, o in zip(scores, numbers)]
        for u, o in enumerate(numbers):
            p, factor = soft[u]
            acc[o] = gain(o, factor, p, vn[u])
        return carry

    lax.fori_loop(0, nz // 2, beside, 0)

    relayed(2 * last)
    relayed(2 * last + 1)
    chunk_keys(last, last % 2)
    keys_last, values_last = kt.at[last % 2], vx.at[last % 2]
    p_odd[...] = jnp.zeros_like(p_odd)
    f_odd[...] = jnp.ones_like(f_odd)

    def result(o, factor, p):
        total = gain(o, factor, p, values_last[...])
        total = total[:, :LANES] / total[:, LANES:]
        return jnp.where(lane_t < HEAD, total[:TOK], total[TOK:]).astype(BF16)

    def finish(i2, carry):
        for u in range(2):
            i = 2 * i2 + u
            o = nz - 1 - i
            s_refs[1 - u][...] = jnp.dot(qx[(o + nz - 1) % nz], keys_last[...], preferred_element_type=F32)
            p, factor = soften(s_refs[u][...], o)
            before = (o + 1) % nz
            back_send[before] = result(before, f_refs[1 - u][...], p_refs[1 - u][...])
            p_refs[u][...] = p
            f_refs[u][...] = factor

            @pl.when(i > 0)
            def _():
                back_copy(before).start()

        return carry

    s_even[...] = jnp.dot(qx[nz - 1], keys_last[...], preferred_element_type=F32)
    lax.fori_loop(0, half, finish, 0)
    back_recv[z] = result(0, f_odd[...], p_odd[...])
    for o in range(1, nz):
        back_wait(o).wait_recv()

    attended = jnp.concatenate([back_recv[k] for k in range(nz)], axis=1)
    wo_copy.wait()
    after = tokens(stream) + jnp.dot(attended, wo[...], preferred_element_type=F32)
    keep(stage, after.astype(BF16).astype(F32))
    for r in range(ROWS):
        for c in range(COLS):
            for t in range(nz):
                grid[r + 1, c + 1, 0:LEVELS, t * LANES : (t + 1) * LANES] = stage[
                    t, pl.ds((r * COLS + c) * LEVELS, LEVELS), :
                ]
    halo_start(1)
    keep(stage, attended.astype(F32))

    def leave(out):
        for l in range(LEVELS):
            for c in range(COLS):
                for t in range(nz):
                    out[l, c, :, t * LANES : (t + 1) * LANES] = stage[
                        t, pl.ds(c * LEVELS + l, ROWS, stride=COLS * LEVELS), :
                    ].astype(BF16)

    leave(att_out)
    halo_end(1)
    conv(conv_b, stage)
    leave(mix_out)

    for which in range(2):
        for i, (a, b, first, rows) in enumerate(SIDES):
            maybe(exists(a), lambda: halo_copy(which, i).wait_send())

    def sent(o, carry):
        @pl.when(o > 0)
        def _():
            q_copy(o).wait_send()
            z_copy(o).wait_send()
            back_copy(o).wait_send()

        for way in range(2):
            y_copy(way, o).wait_send()
            relay_copy(way, o).wait_send()

        @pl.when(has_north)
        def _():
            lat_copy(0, o).wait_send()

        @pl.when(has_south)
        def _():
            lat_copy(1, o).wait_send()

        return carry

    lax.fori_loop(0, nz, sent, 0)


def place(attended, mixed, att_out, mix_out):
    att_out[...] = attended[...]
    mix_out[...] = mixed[...]


def local(nlat, nz, ny, fields, conv_first, w_qkv, w_out, conv_second, key_list, key_count):
    width = fields.shape[-1]
    vmem = pl.BlockSpec(memory_space=pltpu.VMEM)
    smem = pl.BlockSpec(memory_space=pltpu.SMEM)
    hbm = pl.BlockSpec(memory_space=pl.ANY)
    dma = pltpu.SemaphoreType.DMA
    fields = fields.transpose(0, 2, 1, 3)
    out = jax.ShapeDtypeStruct(fields.shape, BF16)
    attended, mixed = pl.pallas_call(
        functools.partial(kernel, nlat, nz, ny),
        out_shape=(out, out),
        in_specs=[vmem, vmem, vmem, smem, smem, hbm, hbm],
        out_specs=(vmem, vmem),
        scratch_shapes=[
            pltpu.VMEM(w_qkv.shape, BF16),
            pltpu.VMEM(w_out.shape, BF16),
            pltpu.VMEM((nz, TOK, LANES), F32),
            pltpu.VMEM((ROWS + 2, COLS + 2, 8, width), F32),
            pltpu.VMEM((nz, TOK, LANES), F32),
            pltpu.VMEM((nz, TOK, LANES), F32),
            pltpu.VMEM((HALO_ROWS, width), F32),
            pltpu.VMEM((2, HALO_ROWS, width), BF16),
            pltpu.VMEM((2, HALO_ROWS, width), BF16),
            pltpu.VMEM((nz, TOK + 16, LANES), BF16),
            pltpu.VMEM((nz, TOK + 16, LANES), BF16),
            pltpu.VMEM((nz, 2 * TOK, LANES), BF16),
            pltpu.VMEM((4 * nz, 2 * TOK, LANES), BF16),
            pltpu.VMEM((2, nz, 2 * TOK, LANES), BF16),
            pltpu.VMEM((nz, 2 * TOK, 2 * LANES), BF16),
            pltpu.VMEM((2, 2 * LANES, CHUNK), BF16),
            pltpu.VMEM((2, CHUNK, 2 * LANES), BF16),
            pltpu.VMEM((2, 2 * TOK, 2 * LANES), BF16),
            pltpu.VMEM((2, 2 * TOK, 2 * LANES), BF16),
            pltpu.VMEM((nz, 2 * TOK, 2 * LANES), F32),
            pltpu.VMEM((nz, 2 * TOK, LANES), F32),
            pltpu.VMEM((2 * TOK, CHUNK), F32),
            pltpu.VMEM((2 * TOK, CHUNK), F32),
            pltpu.VMEM((2 * TOK, CHUNK), BF16),
            pltpu.VMEM((2 * TOK, CHUNK), BF16),
            pltpu.VMEM((2 * TOK, LANES), F32),
            pltpu.VMEM((2 * TOK, LANES), F32),
            pltpu.VMEM((nz, TOK, LANES), BF16),
            pltpu.VMEM((nz, TOK, LANES), BF16),
            dma((2,)),
            dma((2, 8)),
            dma((2, 8)),
            dma((nz,)),
            dma((nz,)),
            dma((nz,)),
            dma((nz,)),
            dma((2, nz)),
            dma((2, nz)),
            dma((2, nz)),
            dma((2, nz)),
            dma((2, nz)),
            dma((2, nz)),
            dma((nz,)),
            dma((nz,)),
        ],
        compiler_params=pltpu.CompilerParams(
            collective_id=0, has_side_effects=True, vmem_limit_bytes=56 * 1024 * 1024
        ),
        name="block",
    )(fields, conv_first, conv_second, key_list, key_count, w_qkv, w_out)
    attended, mixed = pl.pallas_call(
        place,
        out_shape=(out, out),
        in_specs=[vmem, vmem],
        out_specs=(vmem, vmem),
        name="place",
    )(attended, mixed)
    return attended.transpose(0, 2, 1, 3), mixed.transpose(0, 2, 1, 3)


def solution(mesh):
    nlat, nlon = mesh.shape["lat"], mesh.shape["lon"]
    nz = 8
    return jax.shard_map(
        functools.partial(local, nlat, nz, nlon // nz),
        mesh=mesh,
        in_specs=(
            P(None, "lat", "lon", None),
            P(),
            P(),
            P(),
            P(),
            P("lat", "lon", None),
            P("lat", "lon"),
        ),
        out_specs=(P(None, "lat", "lon", None), P(None, "lat", "lon", None)),
        check_vma=False,
    )
```

```python
import functools
import math

import jax
import jax.numpy as jnp
from jax import lax
from jax.experimental import pallas as pl
from jax.experimental.pallas import tpu as pltpu
from jax.sharding import PartitionSpec as P

LEVELS, ROWS, COLS = 4, 4, 9
TOK = LEVELS * ROWS * COLS
HEAD = 64
LANES = 128
CHUNK = 8 * TOK
MARKS = 48
EPSILON = 1e-05
NEG = -1e30
LOW = -3e38
MESH = pl.DeviceIdType.MESH
F32, BF16 = jnp.float32, jnp.bfloat16

SIDES = (
    (-1, 0, 0, 48),
    (1, 0, 48, 48),
    (0, -1, 96, 16),
    (0, 1, 112, 16),
    (-1, -1, 128, 16),
    (-1, 1, 144, 16),
    (1, -1, 160, 16),
    (1, 1, 176, 16),
)
OPPOSITE = (1, 0, 3, 2, 7, 6, 5, 4)
HALO_ROWS = 192


def cells_of(a, b):
    rows = {-1: [1], 1: [ROWS], 0: list(range(1, ROWS + 1))}[a]
    cols = {-1: [1], 1: [COLS], 0: list(range(1, COLS + 1))}[b]
    rim = [(r, c) for r in rows for c in cols]
    return rim, [(r + a, c + b) for r, c in rim]


def kernel(
    nlat, nz, ny,
    fields_in, conv_a_in, conv_b_in, key_list, key_count, w_qkv, w_out,
    att_out, mix_out,
    fields, conv_a, conv_b, wq, wo, flat, grid, stream, stage, halo_f, halo_send, halo_recv,
    q_send, q_recv, kv_send, kv, near, qx, kt, vx, kn, vn, acc, top,
    s_even, s_odd, p_even, p_odd, f_even, f_odd, back_send, back_recv,
    w_sem, hs_sem, hr_sem, qs_sem, qr_sem, zs_sem, zr_sem, ys_sem, yr_sem, rs_sem, rr_sem, ls_sem, lr_sem, bs_sem, br_sem,
):
    lat = lax.axis_index("lat")
    lon = lax.axis_index("lon")
    z = lon // ny
    y = lon % ny
    nlon = nz * ny
    width = nz * LANES
    has_north = lat > 0
    has_south = lat < nlat - 1

    def wrap(i, n):
        return lax.rem(i + n, n)

    def at(zz, yy):
        return (lat, zz * ny + yy)

    fields_copy = pltpu.make_async_copy(fields_in, fields, w_sem.at[2])
    conv_a_copy = pltpu.make_async_copy(conv_a_in, conv_a, w_sem.at[3])
    conv_b_copy = pltpu.make_async_copy(conv_b_in, conv_b, w_sem.at[4])
    fields_copy.start()
    conv_a_copy.start()
    conv_b_copy.start()
    wq_copy = pltpu.make_async_copy(w_qkv, wq, w_sem.at[0])
    wo_copy = pltpu.make_async_copy(w_out, wo, w_sem.at[1])
    wq_copy.start()
    wo_copy.start()

    barrier = pltpu.get_barrier_semaphore()

    def greet(dev):
        pl.semaphore_signal(barrier, inc=1, device_id=dev, device_id_type=MESH)

    for k in range(1, nz):
        greet(at(wrap(z + k, nz), y))
    greet(at(z, wrap(y + 1, ny)))
    greet(at(z, wrap(y - 1, ny)))
    greet((lat, wrap(lon + 1, nlon)))
    greet((lat, wrap(lon - 1, nlon)))

    @pl.when(has_north)
    def _():
        for d in (-1, 0, 1):
            greet((lat - 1, wrap(lon + d, nlon)))

    @pl.when(has_south)
    def _():
        for d in (-1, 0, 1):
            greet((lat + 1, wrap(lon + d, nlon)))

    fields_copy.wait()
    for l in range(LEVELS):
        for c in range(COLS):
            cells = fields[l, c].astype(F32)
            for t in range(nz):
                flat[t, pl.ds((l * COLS + c) * ROWS, ROWS), :] = cells[:, t * LANES : (t + 1) * LANES]
    for r in range(ROWS):
        for c in range(COLS):
            for t in range(nz):
                grid[r + 1, c + 1, 0:LEVELS, t * LANES : (t + 1) * LANES] = flat[
                    t, pl.ds(c * ROWS + r, LEVELS, stride=COLS * ROWS), :
                ]

    def exists(a):
        return {-1: has_north, 0: None, 1: has_south}[a]

    def maybe(cond, fn):
        if cond is None:
            fn()
        else:
            pl.when(cond)(fn)

    def halo_copy(which, i):
        a, b, first, rows = SIDES[i]
        first_there = SIDES[OPPOSITE[i]][2]
        return pltpu.make_async_remote_copy(
            src_ref=halo_send.at[which, pl.ds(first, rows)],
            dst_ref=halo_recv.at[which, pl.ds(first_there, rows)],
            send_sem=hs_sem.at[which, i],
            recv_sem=hr_sem.at[which, OPPOSITE[i]],
            device_id=(lat + a, wrap(lon + b, nlon)),
            device_id_type=MESH,
        )

    def halo_wait(which, i):
        a, b, first, rows = SIDES[i]
        return pltpu.make_async_remote_copy(
            src_ref=halo_send.at[which, pl.ds(first, rows)],
            dst_ref=halo_recv.at[which, pl.ds(first, rows)],
            send_sem=hs_sem.at[which, i],
            recv_sem=hr_sem.at[which, i],
            device_id=(lat + a, wrap(lon + b, nlon)),
            device_id_type=MESH,
        )

    def halo_start(which):
        for i, (a, b, first, rows) in enumerate(SIDES):
            rim, _ = cells_of(a, b)
            for n, (r, c) in enumerate(rim):
                halo_f[pl.ds(first + 4 * n, 4), :] = grid[r, c, 0:LEVELS, :]
            halo_send[which, pl.ds(first, rows), :] = halo_f[pl.ds(first, rows), :].astype(BF16)
            maybe(exists(a), lambda: halo_copy(which, i).start())

    def halo_end(which):
        for i, (a, b, first, rows) in enumerate(SIDES):
            maybe(exists(a), lambda: halo_wait(which, i).wait_recv())
            halo_f[pl.ds(first, rows), :] = halo_recv[which, pl.ds(first, rows), :].astype(F32)
            _, beyond = cells_of(a, b)
            for n, (r, c) in enumerate(beyond):
                value = halo_f[pl.ds(first + 4 * n, 4), :]
                if a != 0:
                    value = jnp.where(exists(a), value, 0.0)
                grid[r, c, 0:LEVELS, :] = value

    def conv(weights, dst):
        chunk = min(256, width)
        for first in range(0, width, chunk):
            lanes = slice(first, first + chunk)
            w = weights[:, lanes]
            for r in range(ROWS):
                total = grid[r + 1, 1 : COLS + 1, 0:LEVELS, lanes]
                for a in range(3):
                    for b in range(3):
                        total = total + w[3 * a + b][None, None, :] * grid[r + a, b : b + COLS, 0:LEVELS, lanes]
                total = total.astype(BF16).astype(F32)
                for c in range(COLS):
                    for t in range(chunk // LANES):
                        dst[first // LANES + t, pl.ds((r * COLS + c) * LEVELS, LEVELS), :] = total[
                            c, :, t * LANES : (t + 1) * LANES
                        ]

    greetings = nz - 1 + 4 + 3 * has_north.astype(jnp.int32) + 3 * has_south.astype(jnp.int32)
    halo_f[...] = jnp.zeros_like(halo_f)
    pl.semaphore_wait(barrier, greetings)
    halo_start(0)

    lane = lax.broadcasted_iota(jnp.int32, (16, LANES), 1)
    count = key_count[0, 0]
    seen = ((lane == nlon) & has_north) | ((lane == nlon + 1) & has_south)
    for s in range(nlon):
        seen = seen | (lane == jnp.where(s < count, key_list[0, 0, s], -1))
    bias = jnp.where(seen, 0.0, NEG).astype(BF16)
    for k in range(nz):
        q_send[k, pl.ds(TOK, 16), :] = bias

    lane_t = lax.broadcasted_iota(jnp.int32, (TOK, LANES), 1)
    ones = jnp.ones((CHUNK, LANES), BF16)
    for u in range(2):
        kt[u, LANES + MARKS :, :] = jnp.zeros((LANES - MARKS, CHUNK), BF16)
        vx[u, :, LANES:] = ones
        vn[u, :, LANES:] = ones[: 2 * TOK]
        for side in range(2):
            kn[u, pl.ds(side * TOK, TOK), LANES:] = jnp.where(lane_t == nlon + side, 1.0, 0.0).astype(BF16)
    vx[1, :, 0:LANES] = jnp.zeros((CHUNK, LANES), BF16)
    p_odd[...] = jnp.zeros_like(p_odd)
    f_odd[...] = jnp.ones_like(f_odd)

    def clear(o, carry):
        top[o] = jnp.full((2 * TOK, LANES), LOW, F32)
        acc[o] = jnp.zeros((2 * TOK, 2 * LANES), F32)
        return carry

    lax.fori_loop(0, nz, clear, 0)

    @pl.when(jnp.logical_not(has_north))
    def _():
        near[0] = jnp.zeros(near.shape[1:], BF16)

    @pl.when(jnp.logical_not(has_south))
    def _():
        near[1] = jnp.zeros(near.shape[1:], BF16)

    halo_end(0)
    conv_a_copy.wait()
    conv(conv_a, stream)

    def tokens(ref):
        return jnp.concatenate([ref[t] for t in range(nz)], axis=1)

    def keep(ref, value):
        for t in range(nz):
            ref[t] = value[:, t * LANES : (t + 1) * LANES]

    x = tokens(stream)
    normed = (x * lax.rsqrt(jnp.mean(x * x, axis=-1, keepdims=True) + EPSILON)).astype(BF16)

    def shift(o):
        odd = o % 2
        return odd * ((o + 1) // 2) + (1 - odd) * ((nz - o // 2) % nz)

    def remote(src, dst, send_sem, recv_sem, dev):
        return pltpu.make_async_remote_copy(
            src_ref=src, dst_ref=dst, send_sem=send_sem, recv_sem=recv_sem, device_id=dev, device_id_type=MESH
        )

    def q_copy(o):
        there = wrap(z + shift(o), nz)
        return remote(q_send.at[there], q_recv.at[o], qs_sem.at[o], qr_sem.at[o], at(there, y))

    def z_copy(o):
        there = wrap(z + shift(o), nz)
        return remote(kv_send.at[there], kv.at[4 * o], zs_sem.at[o], zr_sem.at[o], at(there, y))

    def y_copy(way, o):
        return remote(
            kv.at[4 * o], kv.at[4 * o + 1 + way], ys_sem.at[way, o], yr_sem.at[way, o],
            at(z, wrap(y + 1 - 2 * way, ny)),
        )

    def relay_copy(way, o):
        rows = pl.ds(way * TOK, TOK)
        return remote(
            kv.at[4 * o + 1 + way, rows], kv.at[4 * o + 3, rows], rs_sem.at[way, o], rr_sem.at[way, o],
            at(z, wrap(y + 1 - 2 * way, ny)),
        )

    def lat_copy(way, o):
        return remote(
            kv.at[4 * o], near.at[1 - way, o], ls_sem.at[way, o], lr_sem.at[1 - way, o], (lat - 1 + 2 * way, lon)
        )

    def lat_wait(side, o):
        return remote(kv.at[4 * o], near.at[side, o], ls_sem.at[side, o], lr_sem.at[side, o], (lat - 1 + 2 * side, lon))

    def back_copy(o):
        return remote(
            back_send.at[o], back_recv.at[z], bs_sem.at[o], br_sem.at[o], at(wrap(z - shift(o), nz), y)
        )

    def back_wait(o):
        there = wrap(z + shift(o), nz)
        return remote(back_send.at[o], back_recv.at[there], bs_sem.at[o], br_sem.at[o], at(there, y))

    def project(part, j):
        cols = pl.ds(pl.multiple_of(part * width + j * 256, 256), 256)
        return jnp.dot(normed, wq[:, cols], preferred_element_type=F32)

    scale = HEAD ** -0.5 * math.log2(math.e)
    wq_copy.wait()
    for j in range(nz // 2):
        for part in range(2):
            res = project(1 + part, j).astype(BF16)
            kv_send[2 * j, pl.ds(part * TOK, TOK), :] = res[:, :LANES]
            kv_send[2 * j + 1, pl.ds(part * TOK, TOK), :] = res[:, LANES:]
    for o in range(1, 5):
        z_copy(o).start()
    kv[0] = kv_send[z]

    def forward(o):
        y_copy(0, o).start()
        y_copy(1, o).start()

        @pl.when(has_north)
        def _():
            lat_copy(0, o).start()

        @pl.when(has_south)
        def _():
            lat_copy(1, o).start()

    def relay(o):
        for way in range(2):
            y_copy(way, o).wait_recv()
            relay_copy(way, o).start()

    def relayed(o):
        for way in range(2):
            relay_copy(way, o).wait_recv()

    def arrive(o):
        z_copy(o).wait_recv()
        forward(o)
        if o + 4 < nz:
            z_copy(o + 4).start()

    forward(0)
    for j in range(nz // 2):
        res = (project(0, j) * scale).astype(BF16)
        q_send[2 * j, pl.ds(0, TOK), :] = res[:, :LANES]
        q_send[2 * j + 1, pl.ds(0, TOK), :] = res[:, LANES:]
    for o in range(1, nz):
        q_copy(o).start()
    q_recv[0] = q_send[z]

    def prepare(o, carry):
        @pl.when(o > 0)
        def _():
            q_copy(o).wait_recv()

        q = q_recv[o, pl.ds(0, TOK), :]
        b = jnp.concatenate([q_recv[o, pl.ds(TOK, 16), :]] * (TOK // 16), axis=0)
        zero = jnp.zeros_like(q)
        qx[o, pl.ds(0, TOK), 0:LANES] = jnp.where(lane_t < HEAD, q, zero)
        qx[o, pl.ds(TOK, TOK), 0:LANES] = jnp.where(lane_t < HEAD, zero, q)
        qx[o, pl.ds(0, TOK), LANES:] = b
        qx[o, pl.ds(TOK, TOK), LANES:] = b
        return carry

    def chunk_keys(c, slot):
        keys = jnp.concatenate([kv[8 * c + i, pl.ds(0, TOK), :] for i in range(8)], axis=0)
        kt[slot, 0:LANES, :] = keys.T
        column = lax.broadcasted_iota(jnp.int32, (1, CHUNK), 1)
        number = jnp.zeros((1, CHUNK), jnp.int32)
        for i in range(8):
            yy = (y, wrap(y - 1, ny), wrap(y + 1, ny), wrap(y + 2, ny))[i % 4]
            here = wrap(z - shift(2 * c + i // 4), nz) * ny + yy
            number = jnp.where(column >= i * TOK, here, number)
        row = lax.broadcasted_iota(jnp.int32, (MARKS, CHUNK), 0)
        kt[slot, LANES : LANES + MARKS, :] = jnp.where(row == number, 1.0, 0.0).astype(BF16)
        for i in range(8):
            vx[slot, pl.ds(i * TOK, TOK), 0:LANES] = kv[8 * c + i, pl.ds(TOK, TOK), :]

    def soften(s, o):
        old = top[o]
        new = jnp.maximum(old, jnp.max(s, axis=1, keepdims=True))
        top[o] = new
        return jnp.exp2(s - new[:, :1]).astype(BF16), jnp.exp2(old - new)

    def gain(o, factor, p, values):
        pv = jnp.dot(p, values, preferred_element_type=F32)
        return acc[o] * jnp.concatenate([factor, factor], axis=1) + pv

    chunks = nz // 2
    steps = chunks * nz
    half = nz // 2
    arrive(1)
    relay(0)
    arrive(2)
    relay(1)
    prepare(0, 0)
    relayed(0)
    relayed(1)
    chunk_keys(0, 0)
    if nz > 4:
        plan = {
            0: [(arrive, 3), (relay, 2)],
            1: [(arrive, 4), (relay, 3)],
            2: [(arrive, 5)],
            3: [(relay, 4)],
            4: [(arrive, 6), (relay, 5)],
            5: [(arrive, 7)],
            6: [(relay, 6)],
            8: [(relay, 7)],
        }
        late = []
    else:
        plan = {}
        late = [(relay, 2), (arrive, 3), (relay, 3)]
    s_refs, p_refs, f_refs = (s_even, s_odd), (p_even, p_odd), (f_even, f_odd)

    def advance(t2):
        for when, acts in plan.items():

            @pl.when(t2 == when)
            def _():
                for fn, o in acts:
                    fn(o)

        c = t2 // half

        @pl.when((t2 % half == half - 1) & (c < chunks - 2))
        def _():
            relayed(2 * c + 2)
            relayed(2 * c + 3)
            chunk_keys(c + 1, (c + 1) % 2)

    def pair(t2, carry):
        for i in (1, 2):

            @pl.when(2 * t2 + i < nz)
            def _():
                prepare(2 * t2 + i, 0)

        advance(t2)
        for u in range(2):
            t = 2 * t2 + u
            s_refs[1 - u][...] = jnp.dot(qx[(t + 1) % nz], kt[((t + 1) // nz) % 2], preferred_element_type=F32)
            p, factor = soften(s_refs[u][...], t % nz)
            before = (t + nz - 1) % nz
            acc[before] = gain(before, f_refs[1 - u][...], p_refs[1 - u][...], vx[((t + nz - 1) // nz + 1) % 2])
            p_refs[u][...] = p
            f_refs[u][...] = factor
        return carry

    s_even[...] = jnp.dot(qx[0], kt[0], preferred_element_type=F32)
    lax.fori_loop(0, (chunks - 1) * half, pair, 0)
    acc[nz - 1] = gain(nz - 1, f_odd[...], p_odd[...], vx[(chunks - 2) % 2])
    last = chunks - 1
    for fn, o in late:
        fn(o)

    def beside(i, carry):
        numbers = [2 * i, 2 * i + 1]
        for u, o in enumerate(numbers):
            for side, cond in ((0, has_north), (1, has_south)):

                @pl.when(cond)
                def _():
                    lat_wait(side, o).wait_recv()

        for u, o in enumerate(numbers):
            for side in range(2):
                rows = pl.ds(side * TOK, TOK)
                kn[u, rows, 0:LANES] = near[side, o, pl.ds(0, TOK), :]
                vn[u, rows, 0:LANES] = near[side, o, pl.ds(TOK, TOK), :]
        scores = [
            lax.dot_general(qx[o], kn[u], (((1,), (1,)), ((), ())), preferred_element_type=F32)
            for u, o in enumerate(numbers)
        ]
        soft = [soften(s, o) for s, o in zip(scores, numbers)]
        for u, o in enumerate(numbers):
            p, factor = soft[u]
            acc[o] = gain(o, factor, p, vn[u])
        return carry

    lax.fori_loop(0, nz // 2, beside, 0)

    relayed(2 * last)
    relayed(2 * last + 1)
    chunk_keys(last, last % 2)
    keys_last, values_last = kt.at[last % 2], vx.at[last % 2]
    p_odd[...] = jnp.zeros_like(p_odd)
    f_odd[...] = jnp.ones_like(f_odd)

    def result(o, factor, p):
        total = gain(o, factor, p, values_last[...])
        total = total[:, :LANES] / total[:, LANES:]
        return jnp.where(lane_t < HEAD, total[:TOK], total[TOK:]).astype(BF16)

    def finish(i2, carry):
        for u in range(2):
            i = 2 * i2 + u
            o = nz - 1 - i
            s_refs[1 - u][...] = jnp.dot(qx[(o + nz - 1) % nz], keys_last[...], preferred_element_type=F32)
            p, factor = soften(s_refs[u][...], o)
            before = (o + 1) % nz
            back_send[before] = result(before, f_refs[1 - u][...], p_refs[1 - u][...])
            p_refs[u][...] = p
            f_refs[u][...] = factor

            @pl.when(i > 0)
            def _():
                back_copy(before).start()

        return carry

    s_even[...] = jnp.dot(qx[nz - 1], keys_last[...], preferred_element_type=F32)
    lax.fori_loop(0, half, finish, 0)
    back_recv[z] = result(0, f_odd[...], p_odd[...])
    for o in range(1, nz):
        back_wait(o).wait_recv()

    attended = jnp.concatenate([back_recv[k] for k in range(nz)], axis=1)
    wo_copy.wait()
    after = tokens(stream) + jnp.dot(attended, wo[...], preferred_element_type=F32)
    keep(stage, after.astype(BF16).astype(F32))
    for r in range(ROWS):
        for c in range(COLS):
            for t in range(nz):
                grid[r + 1, c + 1, 0:LEVELS, t * LANES : (t + 1) * LANES] = stage[
                    t, pl.ds((r * COLS + c) * LEVELS, LEVELS), :
                ]
    halo_start(1)
    keep(stage, attended.astype(F32))

    def leave(out):
        for l in range(LEVELS):
            for c in range(COLS):
                for t in range(nz):
                    out[l, c, :, t * LANES : (t + 1) * LANES] = stage[
                        t, pl.ds(c * LEVELS + l, ROWS, stride=COLS * LEVELS), :
                    ].astype(BF16)

    leave(att_out)
    halo_end(1)
    conv_b_copy.wait()
    conv(conv_b, stage)
    leave(mix_out)

    for which in range(2):
        for i, (a, b, first, rows) in enumerate(SIDES):
            maybe(exists(a), lambda: halo_copy(which, i).wait_send())

    def sent(o, carry):
        @pl.when(o > 0)
        def _():
            q_copy(o).wait_send()
            z_copy(o).wait_send()
            back_copy(o).wait_send()

        for way in range(2):
            y_copy(way, o).wait_send()
            relay_copy(way, o).wait_send()

        @pl.when(has_north)
        def _():
            lat_copy(0, o).wait_send()

        @pl.when(has_south)
        def _():
            lat_copy(1, o).wait_send()

        return carry

    lax.fori_loop(0, nz, sent, 0)


def place(attended, mixed, att_out, mix_out):
    att_out[...] = attended[...]
    mix_out[...] = mixed[...]


def local(nlat, nz, ny, fields, conv_first, w_qkv, w_out, conv_second, key_list, key_count):
    width = fields.shape[-1]
    vmem = pl.BlockSpec(memory_space=pltpu.VMEM)
    smem = pl.BlockSpec(memory_space=pltpu.SMEM)
    hbm = pl.BlockSpec(memory_space=pl.ANY)
    dma = pltpu.SemaphoreType.DMA
    fields = fields.transpose(0, 2, 1, 3)
    out = jax.ShapeDtypeStruct(fields.shape, BF16)
    attended, mixed = pl.pallas_call(
        functools.partial(kernel, nlat, nz, ny),
        out_shape=(out, out),
        in_specs=[hbm, hbm, hbm, smem, smem, hbm, hbm],
        out_specs=(vmem, vmem),
        scratch_shapes=[
            pltpu.VMEM(fields.shape, BF16),
            pltpu.VMEM(conv_first.shape, F32),
            pltpu.VMEM(conv_second.shape, F32),
            pltpu.VMEM(w_qkv.shape, BF16),
            pltpu.VMEM(w_out.shape, BF16),
            pltpu.VMEM((nz, TOK, LANES), F32),
            pltpu.VMEM((ROWS + 2, COLS + 2, 8, width), F32),
            pltpu.VMEM((nz, TOK, LANES), F32),
            pltpu.VMEM((nz, TOK, LANES), F32),
            pltpu.VMEM((HALO_ROWS, width), F32),
            pltpu.VMEM((2, HALO_ROWS, width), BF16),
            pltpu.VMEM((2, HALO_ROWS, width), BF16),
            pltpu.VMEM((nz, TOK + 16, LANES), BF16),
            pltpu.VMEM((nz, TOK + 16, LANES), BF16),
            pltpu.VMEM((nz, 2 * TOK, LANES), BF16),
            pltpu.VMEM((4 * nz, 2 * TOK, LANES), BF16),
            pltpu.VMEM((2, nz, 2 * TOK, LANES), BF16),
            pltpu.VMEM((nz, 2 * TOK, 2 * LANES), BF16),
            pltpu.VMEM((2, 2 * LANES, CHUNK), BF16),
            pltpu.VMEM((2, CHUNK, 2 * LANES), BF16),
            pltpu.VMEM((2, 2 * TOK, 2 * LANES), BF16),
            pltpu.VMEM((2, 2 * TOK, 2 * LANES), BF16),
            pltpu.VMEM((nz, 2 * TOK, 2 * LANES), F32),
            pltpu.VMEM((nz, 2 * TOK, LANES), F32),
            pltpu.VMEM((2 * TOK, CHUNK), F32),
            pltpu.VMEM((2 * TOK, CHUNK), F32),
            pltpu.VMEM((2 * TOK, CHUNK), BF16),
            pltpu.VMEM((2 * TOK, CHUNK), BF16),
            pltpu.VMEM((2 * TOK, LANES), F32),
            pltpu.VMEM((2 * TOK, LANES), F32),
            pltpu.VMEM((nz, TOK, LANES), BF16),
            pltpu.VMEM((nz, TOK, LANES), BF16),
            dma((5,)),
            dma((2, 8)),
            dma((2, 8)),
            dma((nz,)),
            dma((nz,)),
            dma((nz,)),
            dma((nz,)),
            dma((2, nz)),
            dma((2, nz)),
            dma((2, nz)),
            dma((2, nz)),
            dma((2, nz)),
            dma((2, nz)),
            dma((nz,)),
            dma((nz,)),
        ],
        compiler_params=pltpu.CompilerParams(
            collective_id=0, has_side_effects=True, vmem_limit_bytes=56 * 1024 * 1024
        ),
        name="block",
    )(fields, conv_first, conv_second, key_list, key_count, w_qkv, w_out)
    attended, mixed = pl.pallas_call(
        place,
        out_shape=(out, out),
        in_specs=[vmem, vmem],
        out_specs=(vmem, vmem),
        name="place",
    )(attended, mixed)
    return attended.transpose(0, 2, 1, 3), mixed.transpose(0, 2, 1, 3)


def solution(mesh):
    nlat, nlon = mesh.shape["lat"], mesh.shape["lon"]
    nz = 8
    return jax.shard_map(
        functools.partial(local, nlat, nz, nlon // nz),
        mesh=mesh,
        in_specs=(
            P(None, "lat", "lon", None),
            P(),
            P(),
            P(),
            P(),
            P("lat", "lon", None),
            P("lat", "lon"),
        ),
        out_specs=(P(None, "lat", "lon", None), P(None, "lat", "lon", None)),
        check_vma=False,
    )
```
